32 devices in a mesh: row: 16 (over z, y, x), col: 2 (over core).
Axes of the slice: x: 2, y: 2, z: 4, core: 2. Of those that a mesh axis runs over, the one named last changes fastest.
Arguments:
- eigvecs: float32 [16384, 4096], P('row', 'col'), may hold values from -6 to 6
- reflectors: float32 [4, 16384, 256], P(None, 'row', 'col'), may hold values from -0.09375 to 0.09375
- factors: float32 [4, 256, 256], P(None, 'col'), may hold values from -2 to 2, as said below
Outputs:
- slab_out: float32 [16384, 4096], P('row', 'col')
The draws below stay inside these ranges and needn't reach their ends.
Inputs may be any that keep to these rules, and one draw needn't show every extreme that they name: Each factors[p] is upper triangular with diagonal between 0.5 and 1.5.
All inputs are finite; a program needn't handle non-finite values.
Results may differ from the reference program's by a relative error of at most 0.00024.
Values sent between devices are 32-bit elements; how exact they have to be, the bound alone decides.
No kernel may reach another device: no remote copies, remote signals or barrier semaphores. Data moves between devices by JAX's collectives and lax.ppermute only.
A program may use at most 128 MiB of HBM per device.

```python
import jax
import jax.numpy as jnp
from jax import lax

NB = 256
NEV = 4096
PANELS = 4
ROWS = 16384


def draw_factors(key, part):
    key = jax.random.fold_in(key, 7)
    first, second = jax.random.split(key)
    rows = jnp.arange(NB)[:, None]
    cols = jnp.arange(NB)[None, :]
    spread = jnp.clip(jax.random.normal(first, (PANELS, NB, NB), jnp.float32) / NB ** 0.5, -2.0, 2.0)
    diag = jax.random.uniform(second, (PANELS, NB, NB), jnp.float32, 0.6, 1.4)
    upper = jnp.where(cols > rows, spread, 0.0)
    return jnp.where(cols == rows, diag, upper).astype(jnp.float32)


def level_of(stream_key, shape, cuts, least, largest):
    level, own = 1.0, jax.random.fold_in(stream_key, 6)
    for axis_at, blocks in cuts:
        heights = jnp.exp(jax.random.uniform(jax.random.fold_in(own, axis_at), (blocks,), jnp.float32, least / len(cuts), largest / len(cuts)))
        level = level * jnp.repeat(heights, shape[axis_at] // blocks).reshape([-1 if axis == axis_at else 1 for axis in range(len(shape))])
    return level


def noise(key, extent, width, most, shards=(), held_as=jnp.bfloat16):
    result = width * jax.random.normal(key, extent, jnp.float32)
    if shards:
        result = result * level_of(key, extent, shards, -0.22, 0.18)
    return jnp.clip(result, -most, most).astype(held_as)


def setup_inputs(seed: int = 0) -> dict:
    streams_of = jax.random.split(jax.random.key(seed), 4)
    return {
        "eigvecs": noise(streams_of[0], (ROWS, NEV), 1.0, 6.0, ((0, 16), (1, 2)), jnp.float32),
        "reflectors": noise(streams_of[1], (PANELS, ROWS, NB), (ROWS // 4) ** -0.5, 0.09375, ((1, 16), (2, 2)), jnp.float32),
        "factors": draw_factors(jax.random.fold_in(streams_of[3], 71), 0),
    }


def reference(eigvecs, reflectors, factors):
    slab = eigvecs
    for position in range(PANELS):
        reflect_block = reflectors[position]
        proj = lax.dot_general(reflect_block, slab, (((0,), (0,)), ((), ())), precision=lax.Precision.HIGHEST, preferred_element_type=jnp.float32)
        weights = jnp.dot(factors[position], proj, precision=lax.Precision.HIGHEST, preferred_element_type=jnp.float32)
        slab = slab - jnp.dot(reflect_block, weights, precision=lax.Precision.HIGHEST, preferred_element_type=jnp.float32)
    return slab
```

```python
import functools

import jax
import jax.numpy as jnp
from jax import lax
from jax.experimental import pallas as pl
from jax.experimental.pallas import tpu as pltpu
from jax.sharding import PartitionSpec as P

LANES = 128
VMEM_LIMIT = 48 * 1024 * 1024


def halves(value):
    high = value.astype(jnp.bfloat16)
    low = (value - high.astype(jnp.float32)).astype(jnp.bfloat16)
    return high, low


def dot(left, right):
    return jnp.dot(left, right, preferred_element_type=jnp.float32)


def dot3(left_high, left_low, right):
    high, low = halves(right)
    return dot(left_high, high) + (dot(left_high, low) + dot(left_low, high))


def exact(left, right):
    return jnp.dot(left, right, precision=lax.Precision.HIGHEST, preferred_element_type=jnp.float32)


def reversed_bits(value, count):
    return sum(((value >> bit) & 1) << (count - 1 - bit) for bit in range(count))


def params(vmem=VMEM_LIMIT):
    return pltpu.CompilerParams(vmem_limit_bytes=vmem)


def pair_table(slots):
    me = lax.axis_index("row") % slots
    half = slots // 2
    count = half.bit_length() - 1
    table = [(me >> 1) ^ reversed_bits(step, count) for step in range(half)]
    return jnp.stack(table + [me & 1]).astype(jnp.int32)


def project_kernel(half, table, blocks_ref, slab_ref, keep0, send0, keep1, send1, high_ref, low_ref):
    step = pl.program_id(0)

    @pl.when(step == 0)
    def _():
        for position in range(2):
            high, low = halves(blocks_ref[position].T)
            high_ref[pl.ds(position * LANES, LANES)] = high
            low_ref[pl.ds(position * LANES, LANES)] = low

    proj = dot3(high_ref[...], low_ref[...], slab_ref[...])
    odd = table[half] == 1
    left, right = proj[:, :LANES], proj[:, LANES:]
    near = jnp.where(odd, right, left)
    far = jnp.where(odd, left, right)
    keep0[0] = near[:LANES]
    send0[0] = far[:LANES]

    @pl.when(step < half // 2)
    def _():
        keep1[0, 0] = near[LANES:]
        keep1[1, 0] = far[LANES:]

    @pl.when(step >= half // 2)
    def _():
        send1[0, 0] = near[LANES:]
        send1[1, 0] = far[LANES:]


def project(table, blocks, first, slab, slots, name):
    rows, columns = slab.shape
    half, quarter = slots // 2, slots // 4
    kind0 = jax.ShapeDtypeStruct((half, LANES, LANES), jnp.float32)
    kind1 = jax.ShapeDtypeStruct((2, quarter, LANES, LANES), jnp.float32)
    spec0 = pl.BlockSpec((1, LANES, LANES), lambda j, t: (j, 0, 0))
    keep1 = pl.BlockSpec((2, 1, LANES, LANES), lambda j, t: (0, jnp.minimum(j, quarter - 1), 0, 0))
    send1 = pl.BlockSpec((2, 1, LANES, LANES), lambda j, t: (0, jnp.maximum(j - quarter, 0), 0, 0))
    out = pl.pallas_call(
        functools.partial(project_kernel, half),
        grid_spec=pltpu.PrefetchScalarGridSpec(
            num_scalar_prefetch=1,
            grid=(half,),
            in_specs=[
                pl.BlockSpec((2, rows, LANES), lambda j, t: (first // 2, 0, 0)),
                pl.BlockSpec((rows, 2 * LANES), lambda j, t: (0, t[j])),
            ],
            out_specs=[spec0, spec0, keep1, send1],
            scratch_shapes=[pltpu.VMEM((2 * LANES, rows), jnp.bfloat16)] * 2,
        ),
        out_shape=[kind0, kind0, kind1, kind1],
        compiler_params=params(),
        cost_estimate=pl.CostEstimate(
            flops=3 * 2 * 2 * LANES * rows * columns, bytes_accessed=4 * rows * columns, transcendentals=0
        ),
        name=name,
    )(table, blocks, slab)
    flat = lambda x: x.reshape(half, LANES, LANES)
    return (out[0], out[1]), (flat(out[2]), flat(out[3]))


def swap(value, bit):
    count = lax.axis_size("row")
    return lax.ppermute(value, "row", [(source, source ^ (1 << bit)) for source in range(count)])


def bits_of(kind, slots):
    order = list(range(slots.bit_length() - 1))
    if kind:
        order[0], order[1] = order[1], order[0]
    return order


def reduce_scatter(pair, kind, slots):
    keep, send = pair
    order = bits_of(kind, slots)
    for bit in order[:-1]:
        got = swap(send, bit)
        half = keep.shape[0] // 2
        keep, send = keep[:half] + got[:half], keep[half:] + got[half:]
    total = keep + swap(send, order[-1])
    for bit in range(len(order), lax.axis_size("row").bit_length() - 1):
        total = total + swap(total, bit)
    return total


def all_gather(block, kind, slots):
    for bit in reversed(bits_of(kind, slots)):
        block = jnp.concatenate([block, swap(block, bit)])
    return block


def solve_kernel(panel, *refs):
    proj0, proj1, factor, gram = refs[:4]
    before, (out0, out1) = refs[4 : 4 + 2 * panel], refs[4 + 2 * panel :]
    proj = jnp.concatenate([proj0[0], proj1[0]])
    if panel:
        proj = proj - exact(gram[...], jnp.concatenate([ref[0] for ref in before]))
    weights = exact(factor[0], proj)
    out0[0] = weights[:LANES]
    out1[0] = weights[LANES:]


def solve(panel, proj, factors, gram, before):
    size = factors.shape[-1]
    block = pl.BlockSpec((1, LANES, LANES), lambda j: (0, 0, 0))
    width = max(panel, 1) * size
    at = panel * (panel - 1) // 2 * size
    return pl.pallas_call(
        functools.partial(solve_kernel, panel),
        grid=(1,),
        in_specs=[
            block,
            block,
            pl.BlockSpec((1, size, size), lambda j: (panel, 0, 0)),
            pl.BlockSpec((size, width), lambda j: (0, 0)),
        ]
        + [block] * len(before),
        out_specs=[block, block],
        out_shape=[jax.ShapeDtypeStruct((1, LANES, LANES), jnp.float32)] * 2,
        compiler_params=params(),
        name=f"solve_panel{panel}",
    )(*proj, factors, gram[:, at : at + width], *before)


def update_kernel(half, kinds, table, blocks0, blocks1, slab_ref, *rest):
    weights, (out_ref, high_ref, low_ref) = rest[:4], rest[4:]

    @pl.when(pl.program_id(0) == 0)
    def _():
        for position, block in enumerate([blocks0[0], blocks0[1], blocks1[0], blocks1[1]]):
            high, low = halves(block)
            high_ref[:, pl.ds(position * LANES, LANES)] = high
            low_ref[:, pl.ds(position * LANES, LANES)] = low

    odd = table[half] == 1
    near = jnp.concatenate([ref[0, 0] if kind == 0 else ref[0, 0, 0] for ref, kind in zip(weights, kinds)])
    far = jnp.concatenate([ref[1, 0] if kind == 0 else ref[0, 1, 0] for ref, kind in zip(weights, kinds)])
    both = jnp.concatenate([jnp.where(odd, far, near), jnp.where(odd, near, far)], axis=1)
    out_ref[...] = slab_ref[...] - dot3(high_ref[...], low_ref[...], both)


def update(table, blocks0, blocks1, first, slab, weights, kinds, slots, name):
    rows, columns = slab.shape
    half, quarter = slots // 2, slots // 4
    column = pl.BlockSpec((rows, 2 * LANES), lambda j, t: (0, t[j]))
    blocks = pl.BlockSpec((2, rows, LANES), lambda j, t: (first // 2, 0, 0))
    specs = [
        pl.BlockSpec((2, 1, LANES, LANES), lambda j, t: (0, j, 0, 0)),
        pl.BlockSpec((1, 2, 1, LANES, LANES), lambda j, t: (j // quarter, 0, j % quarter, 0, 0)),
    ]
    shapes = [(2, half, LANES, LANES), (2, 2, quarter, LANES, LANES)]
    return pl.pallas_call(
        functools.partial(update_kernel, half, kinds),
        grid_spec=pltpu.PrefetchScalarGridSpec(
            num_scalar_prefetch=1,
            grid=(half,),
            in_specs=[blocks, blocks, column] + [specs[kind] for kind in kinds],
            out_specs=column,
            scratch_shapes=[pltpu.VMEM((rows, 4 * LANES), jnp.bfloat16)] * 2,
        ),
        out_shape=jax.ShapeDtypeStruct((rows, columns), jnp.float32),
        compiler_params=params(),
        cost_estimate=pl.CostEstimate(
            flops=3 * 2 * 4 * LANES * rows * columns, bytes_accessed=8 * rows * columns, transcendentals=0
        ),
        name=name,
    )(table, blocks0, blocks1, slab, *[value.reshape(shapes[kind]) for value, kind in zip(weights, kinds)])


def shift(value, step):
    count = lax.axis_size("col")
    return lax.ppermute(value, "col", [((target + step) % count, target) for target in range(count)])


def rotated_gram(own_blocks, blocks):
    parts = []
    for panel in range(1, len(blocks)):
        for other in range(panel):
            parts.append(
                lax.dot_general(
                    own_blocks[panel], blocks[other], (((0,), (0,)), ((), ())),
                    precision=lax.Precision.HIGH, preferred_element_type=jnp.float32,
                )
            )
    return lax.psum(jnp.concatenate(parts, axis=1), "row")


def body(eigvecs, reflectors, factors):
    panels, _, width = reflectors.shape
    size = factors.shape[-1]
    others = size // width
    slots = min(lax.axis_size("row"), eigvecs.shape[1] // LANES)
    table = pair_table(slots)

    pieces = [reflectors] + [shift(reflectors, step) for step in range(1, others)]
    per = others // 2
    join = lambda parts: parts[0] if len(parts) == 1 else jnp.concatenate(parts, axis=2)
    sides = [join(pieces[:per]), join(pieces[per:])]
    factor_rows = jnp.concatenate([factors] + [shift(factors, step) for step in range(1, others)], axis=1)
    start = lax.axis_index("col") * width
    factors = lax.dynamic_slice_in_dim(jnp.concatenate([factor_rows, factor_rows], axis=2), start, size, axis=2)

    chunks = {}
    for first in range(0, panels, 2):
        for side in range(2):
            made = project(table, sides[side], first, eigvecs, slots, f"project_side{side}_panels{first}")
            for kind in range(2):
                chunks[first + kind, side] = (made[kind], kind)

    blocks = [jnp.concatenate([sides[0][panel], sides[1][panel]], axis=1) for panel in range(panels)]
    own = rotated_gram([reflectors[panel] for panel in range(panels)], blocks)
    groups = own.shape[1] // size
    rows = [own]
    for step in range(1, others):
        part = shift(own, step).reshape(width, groups, size)
        rows.append(jnp.roll(part, step * width, axis=2).reshape(width, groups * size))
    gram = jnp.concatenate(rows)

    sums = {at: reduce_scatter(pair, kind, slots) for at, (pair, kind) in chunks.items()}
    before, slab = [], eigvecs
    gathered = {}
    for panel in range(panels):
        weights = solve(panel, [sums[panel, 0], sums[panel, 1]], factors, gram, before)
        before = before + list(weights)
        for side in range(2):
            kind = chunks[panel, side][1]
            gathered[panel, side] = all_gather(weights[side], kind, slots)
    for first in range(0, panels, 2):
        at = [(first, 0), (first + 1, 0), (first, 1), (first + 1, 1)]
        slab = update(
            table, sides[0], sides[1], first, slab, [gathered[key] for key in at], [chunks[key][1] for key in at],
            slots, f"update_panels{first}",
        )
    return slab


def solution(mesh):
    in_specs = (P("row", "col"), P(None, "row", "col"), P(None, "col", None))
    out_specs = P("row", "col")
    return jax.shard_map(body, mesh=mesh, in_specs=in_specs, out_specs=out_specs, check_vma=False)
```

```python
import functools

import jax
import jax.numpy as jnp
from jax import lax
from jax.experimental import pallas as pl
from jax.experimental.pallas import tpu as pltpu
from jax.sharding import PartitionSpec as P

LANES = 128
VMEM_LIMIT = 48 * 1024 * 1024


def halves(value):
    high = value.astype(jnp.bfloat16)
    low = (value - high.astype(jnp.float32)).astype(jnp.bfloat16)
    return high, low


def left_depth(value):
    high, low = halves(value)
    return jnp.concatenate([high, low, high], axis=1)


def right_depth(value):
    high, low = halves(value)
    return jnp.concatenate([high, high, low], axis=0)


def dot(left, right):
    return jnp.dot(left, right, preferred_element_type=jnp.float32)


def exact(left, right):
    return jnp.dot(left, right, precision=lax.Precision.HIGHEST, preferred_element_type=jnp.float32)


def params():
    return pltpu.CompilerParams(vmem_limit_bytes=VMEM_LIMIT)


def order_of(kind, slots):
    order = list(range(slots.bit_length() - 1))
    if kind:
        order[0], order[1] = order[1], order[0]
    return order


def block_of(slot, kind, slots):
    order = order_of(kind, slots)
    return sum(((slot >> (len(order) - 1 - place)) & 1) << bit for place, bit in enumerate(order))


def tables(slots):
    me = lax.axis_index("row") % slots
    half = slots // 2
    pairs = [(me ^ block_of(step, 0, slots)) >> 1 for step in range(half)]
    pieces = [me ^ block_of(slot, 1, slots) for slot in range(slots)]
    return jnp.stack(pairs + [me & 1]).astype(jnp.int32), jnp.stack(pieces).astype(jnp.int32)


def project_kernel(half, side, table, blocks_ref, slab_ref, keep0, send0, keep1, send1, left_ref):
    step = pl.program_id(0)

    @pl.when(step == 0)
    def _():
        for place in range(2):
            left_ref[pl.ds(place * LANES, LANES)] = left_depth(blocks_ref[place ^ side].T)

    proj = dot(left_ref[...], right_depth(slab_ref[...]))
    odd = table[half] == 1
    left, right = proj[:, :LANES], proj[:, LANES:]
    near = jnp.where(odd, right, left)
    far = jnp.where(odd, left, right)
    keep0[0] = near[:LANES]
    send0[0] = far[:LANES]

    @pl.when(step < half // 2)
    def _():
        keep1[0, 0] = near[LANES:]
        keep1[1, 0] = far[LANES:]

    @pl.when(step >= half // 2)
    def _():
        send1[0, 0] = near[LANES:]
        send1[1, 0] = far[LANES:]


def project(table, blocks, side, first, slab, slots):
    rows, columns = slab.shape
    half, quarter = slots // 2, slots // 4
    kind0 = jax.ShapeDtypeStruct((half, LANES, LANES), jnp.float32)
    kind1 = jax.ShapeDtypeStruct((2, quarter, LANES, LANES), jnp.float32)
    spec0 = pl.BlockSpec((1, LANES, LANES), lambda j, t: (j, 0, 0))
    keep1 = pl.BlockSpec((2, 1, LANES, LANES), lambda j, t: (0, jnp.minimum(j, quarter - 1), 0, 0))
    send1 = pl.BlockSpec((2, 1, LANES, LANES), lambda j, t: (0, jnp.maximum(j - quarter, 0), 0, 0))
    out = pl.pallas_call(
        functools.partial(project_kernel, half, side),
        grid_spec=pltpu.PrefetchScalarGridSpec(
            num_scalar_prefetch=1,
            grid=(half,),
            in_specs=[
                pl.BlockSpec((2, rows, LANES), lambda j, t: (first // 2, 0, 0)),
                pl.BlockSpec((rows, 2 * LANES), lambda j, t: (0, t[j])),
            ],
            out_specs=[spec0, spec0, keep1, send1],
            scratch_shapes=[pltpu.VMEM((2 * LANES, 3 * rows), jnp.bfloat16)],
        ),
        out_shape=[kind0, kind0, kind1, kind1],
        compiler_params=params(),
        cost_estimate=pl.CostEstimate(
            flops=3 * 2 * 2 * LANES * rows * columns, bytes_accessed=4 * rows * columns, transcendentals=0
        ),
        name=f"project_side{side}_panels{first}",
    )(table, blocks, slab)
    flat = lambda x: x.reshape(half, LANES, LANES)
    return (out[0], out[1]), (flat(out[2]), flat(out[3]))


def gram_kernel(slots, table, own_ref, side0_ref, side1_ref, keep_ref, send_ref, rows_ref):
    panels, _, width = own_ref.shape
    size = 2 * LANES
    for other in range(panels - 1):
        left = jnp.concatenate([own_ref[panel].T for panel in range(other + 1, panels)])
        right = jnp.concatenate([side0_ref[other], side1_ref[other]], axis=1)
        made = dot(left_depth(left), right_depth(right))
        for place, panel in enumerate(range(other + 1, panels)):
            at = (panel * (panel - 1) // 2 + other) * size
            rows_ref[:, pl.ds(at, size)] = made[place * width : (place + 1) * width]
    tall = width // slots
    for slot in range(slots):
        piece = rows_ref[pl.ds(pl.multiple_of(table[slot] * tall, tall), tall), :]
        out = keep_ref if slot < slots // 2 else send_ref
        for block in range(piece.shape[1] // LANES):
            out[slot % (slots // 2), pl.ds(block * tall, tall)] = piece[:, block * LANES : (block + 1) * LANES]


def gram(pieces, reflectors, sides, slots):
    panels, rows, width = reflectors.shape
    columns = panels * (panels - 1) // 2 * 2 * LANES
    shape = jax.ShapeDtypeStruct((slots // 2, width // slots * (columns // LANES), LANES), jnp.float32)
    return pl.pallas_call(
        functools.partial(gram_kernel, slots),
        grid_spec=pltpu.PrefetchScalarGridSpec(
            num_scalar_prefetch=1,
            grid=(1,),
            in_specs=[pl.BlockSpec(x.shape, lambda j, t: (0, 0, 0)) for x in (reflectors, *sides)],
            out_specs=[pl.BlockSpec(shape.shape, lambda j, t: (0, 0, 0))] * 2,
            scratch_shapes=[pltpu.VMEM((width, columns), jnp.float32)],
        ),
        out_shape=[shape, shape],
        compiler_params=params(),
        cost_estimate=pl.CostEstimate(
            flops=3 * 2 * width * rows * columns, bytes_accessed=12 * rows * panels * LANES, transcendentals=0
        ),
        name="gram_rows",
    )(pieces, reflectors, *sides)


def assemble_kernel(slots, width, table, *refs):
    parts, out = refs[:-1], refs[-1]
    size = 2 * LANES
    tall = width // slots
    for step, part in enumerate(parts):
        for slot in range(slots):
            start = step * width + pl.multiple_of(table[slot] * tall, tall)
            for block in range(out.shape[1] // LANES):
                out[pl.ds(start, tall), pl.ds(block * LANES, LANES)] = part[slot, pl.ds(block * tall, tall)]
        if step:
            for group in range(out.shape[1] // size):
                at = (pl.ds(step * width, width), pl.ds(group * size, size))
                out[at] = pltpu.roll(out[at], step * width, 1)


def assemble(pieces, parts, width, slots):
    tall = width // slots
    columns = parts[0].shape[1] // tall * LANES
    return pl.pallas_call(
        functools.partial(assemble_kernel, slots, width),
        grid_spec=pltpu.PrefetchScalarGridSpec(
            num_scalar_prefetch=1,
            grid=(1,),
            in_specs=[pl.BlockSpec(x.shape, lambda j, t: (0, 0, 0)) for x in parts],
            out_specs=pl.BlockSpec((width * len(parts), columns), lambda j, t: (0, 0)),
        ),
        out_shape=jax.ShapeDtypeStruct((width * len(parts), columns), jnp.float32),
        compiler_params=params(),
        name="assemble_gram",
    )(pieces, *parts)


def swap(value, bit):
    count = lax.axis_size("row")
    return lax.ppermute(value, "row", [(source, source ^ (1 << bit)) for source in range(count)])


def split_sum(keep, got):
    half = keep.shape[0] // 2
    return keep[:half] + got[:half], keep[half:] + got[half:]


def reduce_scatter(pair0, pair1, slots):
    pairs = [pair0, pair1]
    for place in range(2):
        got = [swap(pairs[kind][1], order_of(kind, slots)[place]) for kind in range(2)]
        pairs = [split_sum(pairs[kind][0], got[kind]) if place == 0 else pairs[kind][0] + got[kind] for kind in range(2)]
    total = jnp.concatenate(pairs, axis=1)
    count = slots.bit_length() - 1
    for bit in range(2, count):
        half = total.shape[0] // 2
        total = total[:half] + swap(total[half:], bit)
    for bit in range(count, lax.axis_size("row").bit_length() - 1):
        total = total + swap(total, bit)
    return total


def gather_high(block, slots):
    for bit in reversed(range(2, slots.bit_length() - 1)):
        block = jnp.concatenate([block, swap(block, bit)])
    return block


def gather_low(block, kind, slots):
    for bit in reversed(order_of(kind, slots)[:2]):
        block = jnp.concatenate([block, swap(block, bit)])
    return block


def solve_kernel(panel, *refs):
    proj_ref, factor = refs[:2]
    before, out = refs[3:-1], refs[-1]
    flip = lambda value, at: jnp.concatenate([value[LANES:], value[:LANES]]) if at % 2 else value
    size = 2 * LANES
    proj = flip(proj_ref[0, :size], panel)
    if panel:
        past = jnp.concatenate([flip(ref[0], at) for at, ref in enumerate(before)])
        proj = proj - exact(refs[2][...], past)
    out[0] = flip(exact(factor[0], proj), panel)


def solve(panel, proj, factors, gram_rows, before):
    size = factors.shape[-1]
    block = pl.BlockSpec((1, size, LANES), lambda j: (0, 0, 0))
    width = max(panel, 1) * size
    at = panel * (panel - 1) // 2 * size
    return pl.pallas_call(
        functools.partial(solve_kernel, panel),
        grid=(1,),
        in_specs=[
            pl.BlockSpec(proj.shape, lambda j: (0, 0, 0)),
            pl.BlockSpec((1, size, size), lambda j: (panel, 0, 0)),
            pl.BlockSpec((size, width), lambda j: (0, 0)),
        ]
        + [block] * len(before),
        out_specs=block,
        out_shape=jax.ShapeDtypeStruct((1, size, LANES), jnp.float32),
        compiler_params=params(),
        name=f"solve_panel{panel}",
    )(proj, factors, gram_rows[:, at : at + width], *before)


def update_kernel(half, count, table, *refs):
    blocks, slab_ref, weights = refs[: 2 * count], refs[2 * count], refs[2 * count + 1 : 4 * count + 1]
    out_ref, left_ref = refs[4 * count + 1 :]
    depth = 2 * count * LANES

    @pl.when(pl.program_id(0) == 0)
    def _():
        for place, ref in enumerate(blocks):
            high, low = halves(ref[0])
            for copy, value in enumerate([high, low, high]):
                left_ref[:, pl.ds(copy * depth + place * LANES, LANES)] = value

    odd = table[half] == 1
    near = jnp.concatenate([ref[0, 0, 0] if place % 2 else ref[0, 0] for place, ref in enumerate(weights)])
    far = jnp.concatenate([ref[0, 1, 0] if place % 2 else ref[1, 0] for place, ref in enumerate(weights)])
    both = jnp.concatenate([jnp.where(odd, far, near), jnp.where(odd, near, far)], axis=1)
    out_ref[...] = slab_ref[...] - dot(left_ref[...], right_depth(both))


def update(table, sides, panels, slab, weights, slots):
    rows, columns = slab.shape
    half, quarter = slots // 2, slots // 4
    column = pl.BlockSpec((rows, 2 * LANES), lambda j, t: (0, t[j]))
    block_specs, blocks, weight_specs, values = [], [], [], []
    for panel in panels:
        for kind in range(2):
            block_specs.append(pl.BlockSpec((1, rows, LANES), lambda j, t, panel=panel: (panel, 0, 0)))
            blocks.append(sides[panel % 2 ^ kind])
        weight_specs.append(pl.BlockSpec((2, 1, LANES, LANES), lambda j, t: (0, j, 0, 0)))
        values.append(weights[panel][0].reshape(2, half, LANES, LANES))
        weight_specs.append(pl.BlockSpec((1, 2, 1, LANES, LANES), lambda j, t: (j // quarter, 0, j % quarter, 0, 0)))
        values.append(weights[panel][1].reshape(2, 2, quarter, LANES, LANES))
    depth = 2 * len(panels) * LANES
    return pl.pallas_call(
        functools.partial(update_kernel, half, len(panels)),
        grid_spec=pltpu.PrefetchScalarGridSpec(
            num_scalar_prefetch=1,
            grid=(half,),
            in_specs=block_specs + [column] + weight_specs,
            out_specs=column,
            scratch_shapes=[pltpu.VMEM((rows, 3 * depth), jnp.bfloat16)],
        ),
        out_shape=jax.ShapeDtypeStruct((rows, columns), jnp.float32),
        compiler_params=params(),
        cost_estimate=pl.CostEstimate(
            flops=3 * 2 * depth * rows * columns, bytes_accessed=8 * rows * columns, transcendentals=0
        ),
        name="update_panels" + "".join(map(str, panels)),
    )(table, *blocks, slab, *values)


def shift(value, step):
    count = lax.axis_size("col")
    return lax.ppermute(value, "col", [((target + step) % count, target) for target in range(count)])


def body(eigvecs, reflectors, factors):
    panels, _, width = reflectors.shape
    size = factors.shape[-1]
    others = size // width
    slots = min(lax.axis_size("row"), eigvecs.shape[1] // LANES)
    table, pieces = tables(slots)

    parts = [reflectors] + [shift(reflectors, step) for step in range(1, others)]
    join = lambda some: some[0] if len(some) == 1 else jnp.concatenate(some, axis=2)
    sides = [join(parts[: others // 2]), join(parts[others // 2 :])]
    factor_rows = jnp.concatenate([factors] + [shift(factors, step) for step in range(1, others)], axis=1)
    start = lax.axis_index("col") * width
    factors = lax.dynamic_slice_in_dim(jnp.concatenate([factor_rows, factor_rows], axis=2), start, size, axis=2)

    chunks = {}
    for first in range(0, panels, 2):
        for side in range(2):
            kind0, kind1 = project(table, sides[side], side, first, eigvecs, slots)
            chunks[first + side, 0] = kind0
            chunks[first + 1 - side, 1] = kind1
    gram_pair = gram(pieces, reflectors, sides, slots)
    chunks[0, 1] = tuple(jnp.concatenate([a, b], axis=1) for a, b in zip(chunks[0, 1], gram_pair))

    sums = [reduce_scatter(chunks[panel, 0], chunks[panel, 1], slots) for panel in range(panels)]
    own = gather_low(gather_high(sums[0][:, size:], slots), 1, slots)
    gram_rows = assemble(pieces, [own] + [shift(own, step) for step in range(1, others)], width, slots)

    before, weights = [], []
    for panel in range(panels):
        before.append(solve(panel, sums[panel], factors, gram_rows if panel else factors[0], before))
        high = gather_high(before[panel], slots)
        weights.append([gather_low(high[:, kind * LANES : (kind + 1) * LANES], kind, slots) for kind in range(2)])
    slab = eigvecs
    for some in [list(range(0, panels - 2))] + [[panel] for panel in range(panels - 2, panels)]:
        slab = update(table, sides, some, slab, weights, slots)
    return slab


def solution(mesh):
    in_specs = (P("row", "col"), P(None, "row", "col"), P(None, "col", None))
    out_specs = P("row", "col")
    return jax.shard_map(body, mesh=mesh, in_specs=in_specs, out_specs=out_specs, check_vma=False)
```

```python
import functools

import jax
import jax.numpy as jnp
from jax import lax
from jax.experimental import pallas as pl
from jax.experimental.pallas import tpu as pltpu
from jax.sharding import PartitionSpec as P

LANES = 128
SIZE = 2 * LANES
QUARTERS = 4
VMEM_LIMIT = 40 * 1024 * 1024
F32 = jnp.float32

GROUPS = (
    (((0, 0, 0, 128), (2, 0, 0, 64)), ((1, 0, 0, 128), (2, 0, 64, 128))),
    (((0, 1, 0, 128), (2, 1, 0, 64)), ((1, 1, 0, 128), (2, 1, 64, 128))),
    (((3, 0, 0, 128),), ((3, 1, 0, 128),)),
)
GRAM_GROUP = 1


def rows_of(chunk):
    return sum(last - first for _, _, first, last in chunk)


def pieces_of(panel, side):
    found = []
    for group, chunks in enumerate(GROUPS):
        for kind, chunk in enumerate(chunks):
            row = 0
            for some, of, first, last in chunk:
                if (some, of) == (panel, side):
                    found.append((first, group, kind, row, last - first))
                row += last - first
    return [piece[1:] for piece in sorted(found)]


def schedule(middle):
    if middle == 3:
        return (
            ["p0", "g", "p1", "k1.0", "k1.1", "k2.0", "p2", "k2.1", "k3.0", "k1.2", "k2.2", "k3.1", "k4.0", "k3.2"]
            + ["k5.0", "k4.1", "k4.2", "k6.0", "k5.1", "f.0", "k5.2", "k6.1", "k6.2", "f.1", "u0", "f.2", "u1"]
        )
    groups = range(len(GROUPS))
    steps = [f"k{step}.{group}" for step in range(1, middle + 4) for group in groups]
    return ["p0", "g"] + [f"p{group}" for group in groups[1:]] + steps + ["u0", "u1"]


def halves(value):
    high = value.astype(jnp.bfloat16)
    low = (value - high.astype(F32)).astype(jnp.bfloat16)
    return high, low


def left_depth(value):
    high, low = halves(value)
    return jnp.concatenate([high, low, high], axis=1)


def right_depth(value):
    high, low = halves(value)
    return jnp.concatenate([high, high, low], axis=0)


def dot(left, right):
    return jnp.dot(left, right, preferred_element_type=F32)


def block_of(slot, kind):
    return (slot >> 1) | ((slot & 1) << 1) if kind == 0 else slot


def slot_of(block, kind):
    return block_of(block, kind)


def shape(*dims):
    return jax.ShapeDtypeStruct(dims, F32)


TOKEN = shape(8, LANES)
ANY = pl.BlockSpec(memory_space=pl.ANY)
SMEM = pl.BlockSpec(memory_space=pltpu.SMEM)

COST = pl.CostEstimate(flops=1, bytes_accessed=1, transcendentals=0)


def params():
    return pltpu.CompilerParams(vmem_limit_bytes=VMEM_LIMIT)


def whole(array):
    rank = len(array.shape)
    return pl.BlockSpec(array.shape, lambda *at: (0,) * rank, pipeline_mode=pl.Buffered(1))


def small_call(kernel, name, after, place, ins, outs):
    def run(place_ref, *refs):
        refs = refs[len(after) :]
        kernel(place_ref, refs[: len(ins)], refs[len(ins) : -1])
        refs[-1][...] = jnp.zeros(TOKEN.shape, F32)

    return pl.pallas_call(
        run,
        in_specs=[SMEM] + [ANY] * len(after) + [pl.BlockSpec(memory_space=pltpu.VMEM)] * len(ins),
        out_shape=list(outs) + [TOKEN],
        compiler_params=params(),
        cost_estimate=COST,
        name=name,
    )(place, *after, *ins)


def project_kernel(steps, group, blocks, skip, grams, place, *refs):
    block_refs, slab_ref, refs = refs[skip : skip + len(blocks)], refs[skip + len(blocks)], refs[skip + len(blocks) + 1 :]
    gram_refs, (keep0, send0, keep1, send1, token_out, total) = refs[:grams], refs[grams:]
    step = pl.program_id(0)
    turned = {block: ref[0].T for block, ref in zip(blocks, block_refs)}
    left = left_depth(
        jnp.concatenate([turned[panel, side][first:last] for chunk in group for panel, side, first, last in chunk])
    )
    tall = rows_of(group[0])
    columns = slab_ref.shape[1] // QUARTERS
    for quarter in range(QUARTERS):
        at = pl.ds(quarter * columns, columns)
        made = dot(left, right_depth(slab_ref[:, at]))

        @pl.when(step == 0)
        def _():
            total[:, at] = made

        @pl.when(step > 0)
        def _():
            total[:, at] += made

    @pl.when(step == steps - 1)
    def _():
        token_out[...] = jnp.zeros(TOKEN.shape, F32)
        for kind, outs in enumerate([(keep0, send0), (keep1, send1)]):
            for slot in range(QUARTERS):
                quarter = place[0] ^ block_of(slot, kind)
                part = total[pl.ds(kind * tall, tall), pl.ds(pl.multiple_of(quarter * columns, LANES), columns)]
                out = outs[slot // 2]
                out[slot % 2, :tall] = part
                if grams:
                    out[slot % 2, tall:] = gram_refs[kind][slot]


def project(place, after, sides, group, slab, grams):
    rows, columns = slab.shape
    steps = 4
    deep = rows // steps
    tall = rows_of(group[0]) + (grams[0].shape[1] if grams else 0)
    half = shape(2, tall, columns // QUARTERS)
    spec = pl.BlockSpec(half.shape, lambda j: (0, 0, 0))
    blocks = sorted({(panel, side) for chunk in group for panel, side, _, _ in chunk})
    specs = [pl.BlockSpec((1, deep, LANES), lambda j, panel=panel: (panel, j, 0)) for panel, _ in blocks]
    strip = pl.BlockSpec((deep, columns), lambda j: (j, 0))
    out = pl.pallas_call(
        functools.partial(project_kernel, steps, group, blocks, len(after), len(grams)),
        grid=(steps,),
        in_specs=[SMEM] + [ANY] * len(after) + specs + [strip] + [whole(x) for x in grams],
        out_specs=[spec] * 4 + [pl.BlockSpec(TOKEN.shape, lambda j: (0, 0))],
        scratch_shapes=[pltpu.VMEM((2 * rows_of(group[0]), columns), F32)],
        out_shape=[half] * 4 + [TOKEN],
        compiler_params=params(),
        cost_estimate=COST,
        name="project_" + "_".join(f"{panel}{side}" for panel, side in blocks),
    )(place, *after, *[sides[side] for _, side in blocks], slab, *grams)
    return [(out[0], out[1]), (out[2], out[3])], out[4]


def gram_tiles(rows_shape, piece_shape, quarter, kind):
    (width, wide), (high, columns) = rows_shape, piece_shape
    across, lanes = columns // LANES, wide // LANES
    for tile in range(high // 8 * across):
        row, lane = divmod(kind * (high // 8 * across) + tile, lanes)
        start = pl.multiple_of(quarter * (width // QUARTERS) + 8 * row, 8)
        inside = (pl.ds(tile // across * 8, 8), pl.ds(tile % across * LANES, LANES))
        yield inside, (pl.ds(start, 8), pl.ds(lane * LANES, LANES))


def gram_kernel(place, *refs):
    own_ref, side0_ref, side1_ref, out0, out1, token_out, rows_ref = refs[-7:]
    panels, _, width = own_ref.shape
    for other in range(panels - 1):
        left = jnp.concatenate([own_ref[panel].T for panel in range(other + 1, panels)])
        right = jnp.concatenate([side0_ref[other], side1_ref[other]], axis=1)
        made = dot(left_depth(left), right_depth(right))
        for row, panel in enumerate(range(other + 1, panels)):
            at = (panel * (panel - 1) // 2 + other) * SIZE
            rows_ref[:, pl.ds(at, SIZE)] = made[row * width : (row + 1) * width]
    for kind, out in enumerate([out0, out1]):
        for slot in range(QUARTERS):
            quarter = place[0] ^ block_of(slot, kind)
            for inside, outside in gram_tiles(rows_ref.shape, out.shape[1:], quarter, kind):
                out[(slot, *inside)] = rows_ref[outside]
    token_out[...] = jnp.zeros(TOKEN.shape, F32)


def gram(place, after, reflectors, sides, columns):
    panels, rows, width = reflectors.shape
    wide = panels * (panels - 1) // 2 * SIZE
    out = shape(QUARTERS, width // QUARTERS * (wide // columns) // 2, columns)
    ins = [reflectors, *sides]
    return pl.pallas_call(
        gram_kernel,
        in_specs=[SMEM] + [ANY] * len(after) + [pl.BlockSpec(memory_space=pltpu.VMEM)] * 3,
        scratch_shapes=[pltpu.VMEM((width, wide), F32)],
        out_shape=[out, out, TOKEN],
        compiler_params=params(),
        cost_estimate=COST,
        name="gram_rows",
    )(place, *after, *ins)


def gram_rows_kernel(place, ins, outs):
    (out,) = outs
    above = rows_of(GROUPS[GRAM_GROUP][0])
    _, tall, columns = ins[0].shape
    for kind in range(2):
        for slot in range(QUARTERS):
            ref = ins[2 * kind + slot // 2]
            quarter = place[0] ^ block_of(slot, kind)
            for (rows, lanes), outside in gram_tiles(out.shape, (tall - above, columns), quarter, kind):
                out[outside] = ref[slot % 2, pl.ds(above + rows.start, 8), lanes]


def first_kernel(place, ins, outs):
    for kind in range(2):
        keep, got = ins[2 * kind : 2 * kind + 2]
        for half in range(2):
            outs[2 * kind + half][...] = keep[half] + got[half]


def second_kernel(place, ins, outs):
    for kind in range(2):
        outs[0][kind] = ins[2 * kind][...] + ins[2 * kind + 1][...]


def add_kernel(place, ins, outs):
    outs[0][...] = ins[0][...] + ins[1][...]


def add_split_kernel(place, ins, outs):
    for kind in range(2):
        outs[kind][...] = ins[0][kind] + ins[1][kind]


def take_split_kernel(place, ins, outs):
    outer = place[1] == 1
    for kind in range(2):
        outs[kind][...] = jnp.where(outer, ins[1][kind], ins[0][kind])


def join_kernel(place, ins, outs):
    for kind in range(2):
        for half in range(2):
            outs[kind][half] = ins[2 * kind + half][...]


def update_kernel(panels, last, skip, groups, place, *refs):
    count = len(panels)
    factor_ref, refs = refs[skip], refs[skip + 1 :]
    summed = {group: refs[4 * at : 4 * at + 4] for at, group in enumerate(groups)}
    refs = refs[4 * len(groups) :]
    blocks, slab_ref, extra_ref, out_ref = refs[: 2 * count], *refs[2 * count : 2 * count + 3]
    depth_ref = refs[-1]
    depth = count * SIZE

    def gram_times(panel, past):
        total = None
        for other, weights in enumerate(past):
            start = (panel * (panel - 1) // 2 + other) * SIZE
            term = dot(left_depth(extra_ref[:, pl.ds(start, SIZE)]), weights)
            total = term if total is None else total + term
        return total

    @pl.when(pl.program_id(0) == 0)
    def _():
        columns = summed[groups[0]][0].shape[2]
        for block in range(QUARTERS):
            quarter = place[0] ^ block
            at = pl.ds(pl.multiple_of(quarter * columns, LANES), columns)
            past = []
            for row, panel in enumerate(panels):
                proj = []
                for side in range(2):
                    for group, kind, first, tall in pieces_of(panel, side):
                        slot = slot_of(block, kind)
                        proj.append(summed[group][2 * kind + slot // 2][slot % 2, pl.ds(first, tall)])
                proj = jnp.concatenate(proj)
                if last:
                    proj = proj - extra_ref[:, at]
                elif past:
                    proj = proj - gram_times(panel, past)
                high, low = halves(dot(left_depth(factor_ref[row]), right_depth(proj)))
                past.append(jnp.concatenate([high, high, low]))
                for copy, value in enumerate([high, high, low]):
                    depth_ref[pl.ds(copy * depth + row * SIZE, SIZE), at] = value
            if not last:
                refs[2 * count + 3][:, at] = gram_times(count, past)

    left = left_depth(jnp.concatenate([ref[0] for ref in blocks], axis=1))
    wide = slab_ref.shape[1] // QUARTERS
    for quarter in range(QUARTERS):
        at = pl.ds(quarter * wide, wide)
        out_ref[:, at] = slab_ref[:, at] - dot(left, depth_ref[:, at])


def update(place, after, panels, sides, factors, slab, state, extra, last):
    rows, columns = slab.shape
    steps = 4
    deep = rows // steps
    first, count = panels[0], len(panels)
    size = factors.shape[-1]
    groups = sorted({piece[0] for panel in panels for side in range(2) for piece in pieces_of(panel, side)})
    strip = pl.BlockSpec((deep, columns), lambda j: (j, 0))
    specs, blocks = [], []
    for panel in panels:
        for side in range(2):
            specs.append(pl.BlockSpec((1, deep, LANES), lambda j, panel=panel: (panel, j, 0)))
            blocks.append(sides[side])
    factor = pl.BlockSpec((count, size, size), lambda j: (first // count, 0, 0), pipeline_mode=pl.Buffered(1))
    pieces = [x for group in groups for x in state[group]]
    carry = shape(size, columns)
    outs, out_specs = [shape(rows, columns)], [strip]
    if not last:
        outs, out_specs = outs + [carry], out_specs + [pl.BlockSpec(carry.shape, lambda j: (0, 0))]
    return pl.pallas_call(
        functools.partial(update_kernel, panels, last, len(after), groups),
        grid=(steps,),
        in_specs=[SMEM] + [ANY] * len(after) + [factor] + [whole(x) for x in pieces] + specs + [strip, whole(extra)],
        out_specs=out_specs,
        scratch_shapes=[pltpu.VMEM((3 * count * size, columns), jnp.bfloat16)],
        out_shape=outs,
        compiler_params=params(),
        cost_estimate=COST,
        name="update_panels" + "".join(map(str, panels)),
    )(place, *after, factors, *pieces, *blocks, slab, extra)


def send(value, pairs):
    return lax.ppermute(value, "row", pairs)


def swap(value, bit):
    return send(value, [(source, source ^ (1 << bit)) for source in range(lax.axis_size("row"))])


def shift(value, step):
    count = lax.axis_size("col")
    return lax.ppermute(value, "col", [((target + step) % count, target) for target in range(count)])


def line(value, step):
    moves = [((0, 1), (3, 2)), ((1, 2), (2, 1)), ((1, 0), (2, 3))][step]
    return send(value, [(QUARTERS * a + low, QUARTERS * b + low) for a, b in moves for low in range(QUARTERS)])


def body(eigvecs, reflectors, factors):
    panels, _, width = reflectors.shape
    size = factors.shape[-1]
    others = size // width
    columns = eigvecs.shape[1] // QUARTERS
    count = lax.axis_size("row")
    bits = count.bit_length() - 1
    in_line = bits == 4
    middle = 3 if in_line else bits - 2
    me = lax.axis_index("row")
    level = me // QUARTERS
    outer = ((level == 0) | (level == 3)).astype(jnp.int32)
    place = jnp.stack([me % QUARTERS, outer]).astype(jnp.int32)

    parts = [reflectors] + [shift(reflectors, step) for step in range(1, others)]
    join = lambda some: some[0] if len(some) == 1 else jnp.concatenate(some, axis=2)
    sides = [join(parts[: others // 2]), join(parts[others // 2 :])]
    factor_rows = jnp.concatenate([factors] + [shift(factors, step) for step in range(1, others)], axis=1)
    start = lax.axis_index("col") * width
    factors = lax.dynamic_slice_in_dim(jnp.concatenate([factor_rows, factor_rows], axis=2), start, size, axis=2)

    after = [jnp.zeros(TOKEN.shape, F32)]
    state, grams, slab = {}, [], eigvecs

    def kernel(function, name, ins, outs):
        nonlocal after
        *made, token = small_call(function, name, after, place, ins, outs)
        after = [token]
        return made

    for event in schedule(middle):
        if event[0] == "p":
            group = int(event[1:])
            extra = grams if group == GRAM_GROUP else []
            after = after + ([factors] if group == 1 else [])
            pairs, token = project(place, after, sides, GROUPS[group], eigvecs, extra)
            after = [token]
            state[group] = [pairs[0][0], swap(pairs[0][1], 0), pairs[1][0], swap(pairs[1][1], 1)]
        elif event == "g":
            *grams, token = gram(place, after, reflectors, sides, columns)
            after = [token]
        elif event[0] == "k":
            step, group = map(int, event[1:].split("."))
            held = state[group]
            tall = held[0].shape[-2]
            flat, pair = shape(tall, columns), shape(2, tall, columns)
            if step == 1:
                keep0, send0, keep1, send1 = kernel(first_kernel, f"halve_{group}", held, [flat] * 4)
                state[group] = [keep0, swap(send0, 1), keep1, swap(send1, 0)]
            elif step <= middle + 1:
                function = second_kernel if step == 2 else add_kernel
                (total,) = kernel(function, f"sum{step}_{group}", held, [pair])
                state[group] = [total, line(total, step - 2) if in_line else swap(total, step)]
            elif step == middle + 2:
                function = take_split_kernel if in_line else add_split_kernel
                one, two = kernel(function, f"sum{step}_{group}", held, [flat] * 2)
                state[group] = [one, swap(one, 1), two, swap(two, 0)]
            else:
                one, two = kernel(join_kernel, f"join_{group}", held, [pair] * 2)
                state[group] = [one, swap(one, 0), two, swap(two, 1)]
        elif event[0] == "f":
            after = after + state[int(event[2:])]
        elif event == "u0":
            wide = panels * (panels - 1) // 2 * size
            (own,) = kernel(gram_rows_kernel, "gram_own", state[GRAM_GROUP], [shape(width, wide)])
            rows = [own]
            for step in range(1, others):
                part = shift(own, step).reshape(width, wide // size, size)
                rows.append(jnp.roll(part, step * width, axis=2).reshape(width, wide))
            slab, carry = update(
                place, after, tuple(range(panels - 1)), sides, factors, slab, state, jnp.concatenate(rows), False
            )
        else:
            (slab,) = update(place, after, (panels - 1,), sides, factors, slab, state, carry, True)
    return slab


def solution(mesh):
    in_specs = (P("row", "col"), P(None, "row", "col"), P(None, "col", None))
    out_specs = P("row", "col")
    return jax.shard_map(body, mesh=mesh, in_specs=in_specs, out_specs=out_specs, check_vma=False)
```

```python
import functools

import jax
import jax.numpy as jnp
from jax import lax
from jax.experimental import pallas as pl
from jax.experimental.pallas import tpu as pltpu
from jax.sharding import PartitionSpec as P

LANES = 128
SIZE = 2 * LANES
VMEM_LIMIT = 40 * 1024 * 1024
F32 = jnp.float32

GROUPS = (
    ((0, 0, 0, 128), (1, 0, 0, 64)),
    ((0, 1, 0, 128), (1, 1, 0, 64)),
    ((1, 0, 64, 128), (1, 1, 64, 128), (2, 0, 0, 128)),
    ((2, 1, 0, 128), (3, 0, 0, 128)),
    ((3, 1, 0, 128),),
)
GRAM_GROUP = 1
CALLS = ((0,), (1,), (2,), (3, 4))
UPDATES = ((0, 1), (2,), (3,))
ORDER = (
    ["p0", "g", "p1", "k1.0", "p2", "k2.0", "p3", "k1.1", "k1.2", "k2.1", "k1.3", "k1.4", "k3.0", "k2.2", "k3.1"]
    + ["k3.2", "k2.3", "k2.4", "k4.0", "k3.3", "k4.1", "k3.4", "k4.2", "k5.0", "k4.3", "k6.0", "k5.1", "k4.4"]
    + ["k6.1", "k5.2", "k7.0", "k5.3", "k5.4", "k6.2", "f.0", "k7.1", "k6.3", "k6.4", "k7.2", "f.1", "x", "k7.3"]
    + ["k7.4", "f.2", "u0", "f.3", "u1", "f.4", "u2"]
)


def schedule(steps):
    if steps == 7:
        return ORDER
    groups = range(len(GROUPS))
    order = ["p0", "g"] + [f"p{call}" for call in range(1, len(CALLS))]
    order += [f"k{step}.{group}" for step in range(1, steps + 1) for group in groups]
    return order + ["x"] + [f"u{update}" for update in range(len(UPDATES))]


def rows_of(chunk):
    return sum(last - first for _, _, first, last in chunk)


def pieces_of(panel):
    found = []
    for group, chunk in enumerate(GROUPS):
        row = 0
        for some, side, first, last in chunk:
            if some == panel:
                found.append((side * LANES + first, group, row, last - first))
            row += last - first
    return sorted(found)


def halves(value):
    high = value.astype(jnp.bfloat16)
    low = (value - high.astype(F32)).astype(jnp.bfloat16)
    return high, low


def left_depth(value):
    high, low = halves(value)
    return jnp.concatenate([high, low, high], axis=1)


def right_depth(value):
    high, low = halves(value)
    return jnp.concatenate([high, high, low], axis=0)


def dot(left, right):
    return jnp.dot(left, right, preferred_element_type=F32)


def shape(*dims):
    return jax.ShapeDtypeStruct(dims, F32)


TOKEN = shape(8, LANES)
ANY = pl.BlockSpec(memory_space=pl.ANY)
SMEM = pl.BlockSpec(memory_space=pltpu.SMEM)

COST = pl.CostEstimate(flops=1, bytes_accessed=1, transcendentals=0)


def params():
    return pltpu.CompilerParams(vmem_limit_bytes=VMEM_LIMIT)


def whole(array):
    rank = len(array.shape)
    return pl.BlockSpec(array.shape, lambda *at: (0,) * rank, pipeline_mode=pl.Buffered(1))


def small_call(kernel, name, after, place, ins, outs):
    def run(place_ref, *refs):
        refs = refs[len(after) :]
        kernel(place_ref, refs[: len(ins)], refs[len(ins) : -1])
        refs[-1][...] = jnp.zeros(TOKEN.shape, F32)

    return pl.pallas_call(
        run,
        in_specs=[SMEM] + [ANY] * len(after) + [pl.BlockSpec(memory_space=pltpu.VMEM)] * len(ins),
        out_shape=list(outs) + [TOKEN],
        compiler_params=params(),
        cost_estimate=COST,
        name=name,
    )(place, *after, *ins)


def project_kernel(steps, call, blocks, skip, grams, place, *refs):
    block_refs, slab_ref, refs = refs[skip : skip + len(blocks)], refs[skip + len(blocks)], refs[skip + len(blocks) + 1 :]
    gram_refs, outs, token_out, total = refs[:grams], refs[grams:-2], refs[-2], refs[-1]
    step = pl.program_id(0)
    turned = {block: ref[0].T for block, ref in zip(blocks, block_refs)}
    left = left_depth(
        jnp.concatenate([turned[panel, side][first:last] for group in call for panel, side, first, last in GROUPS[group]])
    )
    wide = slab_ref.shape[1] // 4
    for quarter in range(4):
        at = pl.ds(quarter * wide, wide)
        made = dot(left, right_depth(slab_ref[:, at]))

        @pl.when(step == 0)
        def _():
            total[:, at] = made

        @pl.when(step > 0)
        def _():
            total[:, at] += made

    @pl.when(step == steps - 1)
    def _():
        token_out[...] = jnp.zeros(TOKEN.shape, F32)
        half = outs[0].shape[0]
        above = 0
        for at, group in enumerate(call):
            tall = rows_of(GROUPS[group])
            for slot in range(2 * half):
                out = outs[2 * at + slot // half]
                lanes = pl.ds(pl.multiple_of((place[0] ^ slot) * LANES, LANES), LANES)
                out[slot % half, :tall] = total[pl.ds(above, tall), lanes]
                if gram_refs:
                    out[slot % half, tall:] = gram_refs[0][slot]
            above += tall


def project(place, after, sides, call, slab, grams, slots):
    rows, columns = slab.shape
    steps = 2
    deep = rows // steps
    above = sum(rows_of(GROUPS[group]) for group in call)
    halves_of = []
    for group in call:
        tall = rows_of(GROUPS[group]) + sum(x.shape[1] for x in grams)
        halves_of += [shape(slots // 2, tall, LANES)] * 2
    blocks = sorted({(panel, side) for group in call for panel, side, _, _ in GROUPS[group]})
    specs = [pl.BlockSpec((1, deep, LANES), lambda j, panel=panel: (panel, j, 0)) for panel, _ in blocks]
    strip = pl.BlockSpec((deep, columns), lambda j: (j, 0))
    out = pl.pallas_call(
        functools.partial(project_kernel, steps, call, blocks, len(after), len(grams)),
        grid=(steps,),
        in_specs=[SMEM] + [ANY] * len(after) + specs + [strip] + [whole(x) for x in grams],
        out_specs=[pl.BlockSpec(x.shape, lambda j: (0, 0, 0)) for x in halves_of]
        + [pl.BlockSpec(TOKEN.shape, lambda j: (0, 0))],
        scratch_shapes=[pltpu.VMEM((above, columns), F32)],
        out_shape=halves_of + [TOKEN],
        compiler_params=params(),
        cost_estimate=COST,
        name="project_" + "".join(map(str, call)),
    )(place, *after, *[sides[side] for _, side in blocks], slab, *grams)
    return [(out[2 * at], out[2 * at + 1]) for at in range(len(call))], out[-1]


def gram_kernel(place, *refs):
    own_ref, side0_ref, side1_ref, out, token_out, rows_ref = refs[-6:]
    panels, _, width = own_ref.shape
    for other in range(panels - 1):
        left = jnp.concatenate([own_ref[panel].T for panel in range(other + 1, panels)])
        right = jnp.concatenate([side0_ref[other], side1_ref[other]], axis=1)
        made = dot(left_depth(left), right_depth(right))
        for row, panel in enumerate(range(other + 1, panels)):
            at = (panel * (panel - 1) // 2 + other) * SIZE
            rows_ref[:, pl.ds(at, SIZE)] = made[row * width : (row + 1) * width]
    slots = out.shape[0]
    tall = width // slots
    for slot in range(slots):
        rows = pl.ds(pl.multiple_of((place[0] ^ slot) * tall, tall), tall)
        for block in range(rows_ref.shape[1] // LANES):
            out[slot, pl.ds(block * tall, tall)] = rows_ref[rows, pl.ds(block * LANES, LANES)]
    token_out[...] = jnp.zeros(TOKEN.shape, F32)


def gram(place, after, reflectors, sides, slots):
    panels, _, width = reflectors.shape
    wide = panels * (panels - 1) // 2 * SIZE
    ins = [reflectors, *sides]
    return pl.pallas_call(
        gram_kernel,
        in_specs=[SMEM] + [ANY] * len(after) + [pl.BlockSpec(memory_space=pltpu.VMEM)] * 3,
        scratch_shapes=[pltpu.VMEM((width, wide), F32)],
        out_shape=[shape(slots, width // slots * (wide // LANES), LANES), TOKEN],
        compiler_params=params(),
        cost_estimate=COST,
        name="gram_rows",
    )(place, *after, *ins)


def gram_rows_kernel(place, ins, outs):
    (out,) = outs
    above = rows_of(GROUPS[GRAM_GROUP])
    half = ins[0].shape[0]
    tall = out.shape[0] // (2 * half)
    for slot in range(2 * half):
        rows = pl.ds(pl.multiple_of((place[0] ^ slot) * tall, tall), tall)
        for block in range(out.shape[1] // LANES):
            out[rows, pl.ds(block * LANES, LANES)] = ins[slot // half][slot % half, pl.ds(above + block * tall, tall)]


def halve_kernel(place, ins, outs):
    keep, got = ins
    half = outs[0].shape[0]
    outs[0][...] = keep[:half] + got[:half]
    outs[1][...] = keep[half:] + got[half:]


def add_kernel(place, ins, outs):
    outs[0][...] = ins[0][...] + ins[1][...]


def join_kernel(place, ins, outs):
    half = ins[0].shape[0]
    outs[0][:half] = ins[0][...]
    outs[0][half:] = ins[1][...]


def update_kernel(panels, parts, carried, left_over, skip, groups, place, *refs):
    count = len(panels)
    factor_ref, refs = refs[skip], refs[skip + 1 :]
    summed = {group: refs[2 * at : 2 * at + 2] for at, group in enumerate(groups)}
    refs = refs[2 * len(groups) :]
    gram_refs, refs = refs[:parts], refs[parts:]
    carry_ref, refs = (refs[0], refs[1:]) if carried else (None, refs)
    blocks, slab_ref, out_ref = refs[: 2 * count], refs[2 * count], refs[2 * count + 1]
    depth_ref, proj_ref = refs[-2:]
    depth = count * SIZE
    columns = slab_ref.shape[1]
    wide = columns // 4

    def gram_block(panel, other):
        at = pl.ds((panel * (panel - 1) // 2 + other) * SIZE, SIZE)
        width = gram_refs[0].shape[0]
        rows = [ref[:, at] for ref in gram_refs]
        return jnp.concatenate([pltpu.roll(part, step * width, 1) if step else part for step, part in enumerate(rows)])

    @pl.when(pl.program_id(0) == 0)
    def _():
        for row, panel in enumerate(panels):
            for at, group, first, tall in pieces_of(panel):
                half = summed[group][0].shape[0]
                for slot in range(2 * half):
                    lanes = pl.ds(pl.multiple_of((place[0] ^ slot) * LANES, LANES), LANES)
                    proj_ref[pl.ds(row * SIZE + at, tall), lanes] = summed[group][slot // half][
                        slot % half, pl.ds(first, tall)
                    ]
        factor = [left_depth(factor_ref[row]) for row in range(count)]
        later = [panels[-1] + 1 + more for more in range(left_over)]
        grams = {
            (panel, row): left_depth(gram_block(panel, panels[row]))
            for panel in list(panels) + later
            for row in range(count)
            if panels[row] < panel
        }
        for quarter in range(4):
            at = pl.ds(quarter * wide, wide)
            past = []

            def less(value, panel, sign):
                for row, weights in enumerate(past):
                    value = value + sign * dot(grams[panel, row], weights)
                return value

            for row in range(count):
                proj = proj_ref[pl.ds(row * SIZE, SIZE), at]
                if carried:
                    proj = proj - carry_ref[pl.ds(row * SIZE, SIZE), at]
                proj = less(proj, panels[row], -1.0)
                high, low = halves(dot(factor[row], right_depth(proj)))
                past.append(jnp.concatenate([high, high, low]))
                for copy, value in enumerate([high, high, low]):
                    depth_ref[pl.ds(copy * depth + row * SIZE, SIZE), at] = value
            for more, panel in enumerate(later):
                value = carry_ref[pl.ds((count + more) * SIZE, SIZE), at] if carried else jnp.zeros((SIZE, wide), F32)
                refs[2 * count + 2][pl.ds(more * SIZE, SIZE), at] = less(value, panel, 1.0)

    left = left_depth(jnp.concatenate([ref[0] for ref in blocks], axis=1))
    for quarter in range(4):
        at = pl.ds(quarter * wide, wide)
        out_ref[:, at] = slab_ref[:, at] - dot(left, depth_ref[:, at])


def update(place, after, panels, left_over, sides, factors, slab, state, grams, carry):
    rows, columns = slab.shape
    steps = 4
    deep = rows // steps
    first, count = panels[0], len(panels)
    size = factors.shape[-1]
    groups = sorted({piece[1] for panel in panels for piece in pieces_of(panel)})
    strip = pl.BlockSpec((deep, columns), lambda j: (j, 0))
    specs, blocks = [], []
    for panel in panels:
        for side in range(2):
            specs.append(pl.BlockSpec((1, deep, LANES), lambda j, panel=panel: (panel, j, 0)))
            blocks.append(sides[side])
    factor = pl.BlockSpec((count, size, size), lambda j: (first // count, 0, 0), pipeline_mode=pl.Buffered(1))
    grams = grams if left_over or count > 1 else []
    carries = [] if carry is None else [carry]
    constant = [x for group in groups for x in state[group]] + list(grams) + carries
    outs, out_specs = [shape(rows, columns)], [strip]
    if left_over:
        outs.append(shape(left_over * size, columns))
        out_specs.append(pl.BlockSpec(outs[1].shape, lambda j: (0, 0)))
    made = pl.pallas_call(
        functools.partial(update_kernel, panels, len(grams), len(carries), left_over, len(after), groups),
        grid=(steps,),
        in_specs=[SMEM] + [ANY] * len(after) + [factor] + [whole(x) for x in constant] + specs + [strip],
        out_specs=out_specs,
        scratch_shapes=[pltpu.VMEM((3 * count * size, columns), jnp.bfloat16), pltpu.VMEM((count * size, columns), F32)],
        out_shape=outs,
        compiler_params=params(),
        cost_estimate=COST,
        name="update_panels" + "".join(map(str, panels)),
    )(place, *after, factors, *constant, *blocks, slab)
    return made[0], made[1] if left_over else None


def order_of(kind, bits):
    first, second = (0, 1) if kind == 0 else (1, 0)
    order = [first, 2, second] + list(range(3, bits)) if bits > 2 else [first, second]
    return order[:bits]


def swap(value, step):
    rows, cores = lax.axis_size("row"), lax.axis_size("col")
    bits = rows.bit_length() - 1
    pairs = [
        (row * cores + core, (row ^ (1 << order_of(core % 2, bits)[step])) * cores + core)
        for row in range(rows)
        for core in range(cores)
    ]
    return lax.ppermute(value, ("row", "col"), pairs)


def shift(value, step):
    count = lax.axis_size("col")
    return lax.ppermute(value, "col", [((target + step) % count, target) for target in range(count)])


def body(eigvecs, reflectors, factors):
    panels, _, width = reflectors.shape
    size = factors.shape[-1]
    others = size // width
    bits = lax.axis_size("row").bit_length() - 1
    slots = min(lax.axis_size("row"), eigvecs.shape[1] // LANES)
    cuts = slots.bit_length() - 1
    me, core = lax.axis_index("row"), lax.axis_index("col")
    own = [
        sum(((me >> bit) & 1) << (cuts - 1 - at) for at, bit in enumerate(order_of(kind, bits)[:cuts])) for kind in range(2)
    ]
    place = jnp.stack([jnp.where(core % 2 == 0, own[0], own[1])]).astype(jnp.int32)

    parts = [reflectors] + [shift(reflectors, step) for step in range(1, others)]
    join = lambda some: some[0] if len(some) == 1 else jnp.concatenate(some, axis=2)
    sides = [join(parts[: others // 2]), join(parts[others // 2 :])]
    factor_rows = jnp.concatenate([factors] + [shift(factors, step) for step in range(1, others)], axis=1)
    factors = lax.dynamic_slice_in_dim(jnp.concatenate([factor_rows, factor_rows], axis=2), core * width, size, axis=2)

    after = [jnp.zeros(TOKEN.shape, F32)]
    state, grams, slab, carry = {}, [], eigvecs, None

    def kernel(function, name, ins, outs):
        nonlocal after
        *made, token = small_call(function, name, after, place, ins, outs)
        after = [token]
        return made

    for event in schedule(bits + cuts - 1):
        if event[0] == "p":
            call = CALLS[int(event[1:])]
            after = after + ([factors] if event == "p1" else [])
            made, token = project(place, after, sides, call, eigvecs, grams if call == (GRAM_GROUP,) else [], slots)
            after = [token]
            for group, (keep, send) in zip(call, made):
                state[group] = [keep, swap(send, 0)]
        elif event == "g":
            rows, token = gram(place, after, reflectors, sides, slots)
            grams, after = [rows], [token]
        elif event[0] == "k":
            step, group = map(int, event[1:].split("."))
            held = state[group]
            wide, tall, _ = held[0].shape
            if step < cuts:
                keep, send = kernel(halve_kernel, f"halve{step}_{group}", held, [shape(wide // 2, tall, LANES)] * 2)
                state[group] = [keep, swap(send, step)]
            elif step <= bits:
                (total,) = kernel(add_kernel, f"sum{step}_{group}", held, [shape(*held[0].shape)])
                state[group] = [total, swap(total, step if step < bits else cuts - 1)]
            else:
                (block,) = kernel(join_kernel, f"join{step}_{group}", held, [shape(2 * wide, tall, LANES)])
                state[group] = [block, swap(block, cuts - 1 - (step - bits))]
        elif event[0] == "f":
            after = after + [state[int(event[2:])][1]]
        elif event == "x":
            wide = panels * (panels - 1) // 2 * size
            (rows,) = kernel(gram_rows_kernel, "gram_own", state[GRAM_GROUP], [shape(width, wide)])
            grams = [rows] + [shift(rows, step) for step in range(1, others)]
        else:
            some = UPDATES[int(event[1:])]
            slab, carry = update(
                place, after, some, panels - 1 - some[-1], sides, factors, slab, state, grams, carry
            )
            after = [slab]
    return slab


def solution(mesh):
    in_specs = (P("row", "col"), P(None, "row", "col"), P(None, "col", None))
    out_specs = P("row", "col")
    return jax.shard_map(body, mesh=mesh, in_specs=in_specs, out_specs=out_specs, check_vma=False)
```

```python
import functools

import jax
import jax.numpy as jnp
from jax import lax
from jax.experimental import pallas as pl
from jax.experimental.pallas import tpu as pltpu
from jax.sharding import PartitionSpec as P

LANES = 128
SIZE = 2 * LANES
VMEM_LIMIT = 40 * 1024 * 1024
F32 = jnp.float32

GROUPS = (
    ((0, 0, 0, 128), (1, 0, 0, 64)),
    ((0, 1, 0, 128), (1, 1, 0, 64)),
    ((1, 0, 64, 128), (1, 1, 64, 128), (2, 0, 0, 128)),
    ((2, 1, 0, 128), (3, 0, 0, 128)),
    ((3, 1, 0, 128),),
)
GRAM_GROUP = 1
CALLS = ((0,), (1,), (2,), (3, 4))
ORDER = (
    ["p0", "g", "p1", "k1.0", "p2", "k2.0", "k1.1", "p3", "k1.2", "k2.1", "k3.0", "k1.3", "k1.4", "k2.2", "k3.1"]
    + ["k3.2", "k2.3", "k4.0", "k2.4", "k3.3", "k4.1", "k3.4", "k4.2", "k5.0", "k4.3", "k6.0", "k5.1", "k4.4"]
    + ["k5.2", "k6.1", "k7.0", "k5.3", "k6.2", "k5.4", "f.0", "k7.1", "k6.4", "k6.3", "u0a", "k7.2", "k7.4", "f.1"]
    + ["x", "u0b", "u1a", "f.2", "k7.3", "u1b", "f.4", "u2a", "u3a", "f.3", "u2b", "u3b"]
)


def schedule(steps, panels):
    if steps == 7:
        return ORDER
    groups = range(len(GROUPS))
    order = ["p0", "g"] + [f"p{call}" for call in range(1, len(CALLS))]
    order += [f"k{step}.{group}" for step in range(1, steps + 1) for group in groups]
    return order + ["x"] + [f"u{panel}{half}" for panel in range(panels) for half in "ab"]


def rows_of(chunk):
    return sum(last - first for _, _, first, last in chunk)


def pieces_of(panel):
    found = []
    for group, chunk in enumerate(GROUPS):
        row = 0
        for some, side, first, last in chunk:
            if some == panel:
                found.append((side * LANES + first, group, row, last - first))
            row += last - first
    return sorted(found)


def halves(value):
    high = value.astype(jnp.bfloat16)
    low = (value - high.astype(F32)).astype(jnp.bfloat16)
    return high, low


def left_depth(value):
    high, low = halves(value)
    return jnp.concatenate([high, low, high], axis=1)


def right_depth(value):
    high, low = halves(value)
    return jnp.concatenate([high, high, low], axis=0)


def dot(left, right):
    return jnp.dot(left, right, preferred_element_type=F32)


def shape(*dims):
    return jax.ShapeDtypeStruct(dims, F32)


TOKEN = shape(8, LANES)
ANY = pl.BlockSpec(memory_space=pl.ANY)
SMEM = pl.BlockSpec(memory_space=pltpu.SMEM)

COST = pl.CostEstimate(flops=10**12, bytes_accessed=100, transcendentals=0)


def params():
    return pltpu.CompilerParams(vmem_limit_bytes=VMEM_LIMIT)


def whole(array):
    rank = len(array.shape)
    return pl.BlockSpec(array.shape, lambda *at: (0,) * rank, pipeline_mode=pl.Buffered(1))


def small_call(kernel, name, after, place, ins, outs):
    def run(place_ref, *refs):
        refs = refs[len(after) :]
        kernel(place_ref, refs[: len(ins)], refs[len(ins) : -1])
        refs[-1][...] = jnp.zeros(TOKEN.shape, F32)

    return pl.pallas_call(
        run,
        in_specs=[SMEM] + [ANY] * len(after) + [pl.BlockSpec(memory_space=pltpu.VMEM)] * len(ins),
        out_shape=list(outs) + [TOKEN],
        compiler_params=params(),
        cost_estimate=COST,
        name=name,
    )(place, *after, *ins)


def project_kernel(steps, call, blocks, skip, grams, place, *refs):
    block_refs, slab_ref, refs = refs[skip : skip + len(blocks)], refs[skip + len(blocks)], refs[skip + len(blocks) + 1 :]
    gram_refs, outs, token_out, total = refs[:grams], refs[grams:-2], refs[-2], refs[-1]
    step = pl.program_id(0)
    turned = {block: ref[0].T for block, ref in zip(blocks, block_refs)}
    left = left_depth(
        jnp.concatenate([turned[panel, side][first:last] for group in call for panel, side, first, last in GROUPS[group]])
    )
    wide = slab_ref.shape[1] // 4
    for quarter in range(4):
        at = pl.ds(quarter * wide, wide)
        made = dot(left, right_depth(slab_ref[:, at]))

        @pl.when(step == 0)
        def _():
            total[:, at] = made

        @pl.when(step > 0)
        def _():
            total[:, at] += made

    @pl.when(step == steps - 1)
    def _():
        token_out[...] = jnp.zeros(TOKEN.shape, F32)
        half = outs[0].shape[0]
        above = 0
        for at, group in enumerate(call):
            tall = rows_of(GROUPS[group])
            for slot in range(2 * half):
                out = outs[2 * at + slot // half]
                lanes = pl.ds(pl.multiple_of((place[0] ^ slot) * LANES, LANES), LANES)
                out[slot % half, :tall] = total[pl.ds(above, tall), lanes]
                if gram_refs:
                    out[slot % half, tall:] = gram_refs[0][slot]
            above += tall


def project(place, after, sides, call, slab, grams, slots):
    rows, columns = slab.shape
    steps = 2
    deep = rows // steps
    above = sum(rows_of(GROUPS[group]) for group in call)
    halves_of = []
    for group in call:
        tall = rows_of(GROUPS[group]) + sum(x.shape[1] for x in grams)
        halves_of += [shape(slots // 2, tall, LANES)] * 2
    blocks = sorted({(panel, side) for group in call for panel, side, _, _ in GROUPS[group]})
    specs = [pl.BlockSpec((1, deep, LANES), lambda j, panel=panel: (panel, j, 0)) for panel, _ in blocks]
    strip = pl.BlockSpec((deep, columns), lambda j: (j, 0))
    out = pl.pallas_call(
        functools.partial(project_kernel, steps, call, blocks, len(after), len(grams)),
        grid=(steps,),
        in_specs=[SMEM] + [ANY] * len(after) + specs + [strip] + [whole(x) for x in grams],
        out_specs=[pl.BlockSpec(x.shape, lambda j: (0, 0, 0)) for x in halves_of]
        + [pl.BlockSpec(TOKEN.shape, lambda j: (0, 0))],
        scratch_shapes=[pltpu.VMEM((above, columns), F32)],
        out_shape=halves_of + [TOKEN],
        compiler_params=params(),
        cost_estimate=COST,
        name="project_" + "".join(map(str, call)),
    )(place, *after, *[sides[side] for _, side in blocks], slab, *grams)
    return [(out[2 * at], out[2 * at + 1]) for at in range(len(call))], out[-1]


def gram_kernel(place, *refs):
    own_ref, side0_ref, side1_ref, out, token_out, rows_ref = refs[-6:]
    panels, _, width = own_ref.shape
    for other in range(panels - 1):
        left = jnp.concatenate([own_ref[panel].T for panel in range(other + 1, panels)])
        right = jnp.concatenate([side0_ref[other], side1_ref[other]], axis=1)
        made = dot(left_depth(left), right_depth(right))
        for row, panel in enumerate(range(other + 1, panels)):
            at = (panel * (panel - 1) // 2 + other) * SIZE
            rows_ref[:, pl.ds(at, SIZE)] = made[row * width : (row + 1) * width]
    slots = out.shape[0]
    tall = width // slots
    for slot in range(slots):
        rows = pl.ds(pl.multiple_of((place[0] ^ slot) * tall, tall), tall)
        for block in range(rows_ref.shape[1] // LANES):
            out[slot, pl.ds(block * tall, tall)] = rows_ref[rows, pl.ds(block * LANES, LANES)]
    token_out[...] = jnp.zeros(TOKEN.shape, F32)


def gram(place, after, reflectors, sides, slots):
    panels, _, width = reflectors.shape
    wide = panels * (panels - 1) // 2 * SIZE
    ins = [reflectors, *sides]
    return pl.pallas_call(
        gram_kernel,
        in_specs=[SMEM] + [ANY] * len(after) + [pl.BlockSpec(memory_space=pltpu.VMEM)] * 3,
        scratch_shapes=[pltpu.VMEM((width, wide), F32)],
        out_shape=[shape(slots, width // slots * (wide // LANES), LANES), TOKEN],
        compiler_params=params(),
        cost_estimate=COST,
        name="gram_rows",
    )(place, *after, *ins)


def gram_rows_kernel(place, ins, outs):
    (out,) = outs
    above = rows_of(GROUPS[GRAM_GROUP])
    half = ins[0].shape[0]
    tall = out.shape[0] // (2 * half)
    for slot in range(2 * half):
        rows = pl.ds(pl.multiple_of((place[0] ^ slot) * tall, tall), tall)
        for block in range(out.shape[1] // LANES):
            out[rows, pl.ds(block * LANES, LANES)] = ins[slot // half][slot % half, pl.ds(above + block * tall, tall)]


def halve_kernel(place, ins, outs):
    keep, got = ins
    half = outs[0].shape[0]
    outs[0][...] = keep[:half] + got[:half]
    outs[1][...] = keep[half:] + got[half:]


def add_kernel(place, ins, outs):
    outs[0][...] = ins[0][...] + ins[1][...]


def join_kernel(place, ins, outs):
    half = ins[0].shape[0]
    outs[0][:half] = ins[0][...]
    outs[0][half:] = ins[1][...]


def update_kernel(panel, counts, place, *refs):
    refs = list(refs)
    take = lambda count: [refs.pop(0) for _ in range(count)]
    take(counts["after"])
    (factor_ref,) = take(1)
    summed = take(counts["groups"])
    gram_refs, past_refs, carry_refs = take(counts["grams"]), take(counts["past"]), take(counts["carry"])
    blocks, (slab_ref,) = take(2), take(1)
    take(counts["target"])
    (out_ref,), extra_out, (token_out,) = take(1), take(counts["extra"]), take(1)
    depth_ref, proj_ref = refs
    columns = slab_ref.shape[1]
    wide = columns // 2

    def gram_block(panel, other):
        at = pl.ds((panel * (panel - 1) // 2 + other) * SIZE, SIZE)
        width = gram_refs[0].shape[0]
        rows = [ref[:, at] for ref in gram_refs]
        return left_depth(
            jnp.concatenate([pltpu.roll(part, step * width, 1) if step else part for step, part in enumerate(rows)])
        )

    @pl.when(pl.program_id(0) == 0)
    def _():
        token_out[...] = jnp.zeros(TOKEN.shape, F32)
        groups = groups_of(panel)
        for at, group, first, tall in pieces_of(panel):
            ref = summed[groups.index(group)]
            half = ref.shape[0]
            for slot in range(half):
                lanes = pl.ds(pl.multiple_of(((place[0] ^ slot) & (half - 1)) * LANES, LANES), LANES)
                proj_ref[pl.ds(at, tall), lanes] = ref[slot, pl.ds(first, tall)]
        factor = left_depth(factor_ref[0])
        before = [gram_block(panel, other) for other in range(counts["past"])]
        later = list(range(panel + 1, panel + 1 + extra_out[0].shape[0] // SIZE)) if gram_refs else []
        grams = {more: [gram_block(more, other) for other in range(panel - counts["past"], panel + 1)] for more in later}
        for side in range(2):
            at = pl.ds(side * wide, wide)
            proj = proj_ref[:, at]
            if carry_refs:
                proj = proj - carry_refs[0][:SIZE, at]
            for other, block in enumerate(before):
                proj = proj - dot(block, past_refs[other][:, at])
            high, low = halves(dot(factor, right_depth(proj)))
            weights = jnp.concatenate([high, high, low])
            depth_ref[:, at] = weights
            if extra_out and not gram_refs:
                extra_out[0][:, at] = weights
            for row, more in enumerate(later):
                terms = [ref[:, at] for ref in past_refs] + [weights]
                value = sum(dot(block, term) for block, term in zip(grams[more], terms))
                if carry_refs:
                    value = value + carry_refs[0][pl.ds((row + 1) * SIZE, SIZE), at]
                extra_out[0][pl.ds(row * SIZE, SIZE), at] = value

    left = left_depth(jnp.concatenate([ref[0] for ref in blocks], axis=1))
    for side in range(2):
        at = pl.ds(side * wide, wide)
        out_ref[:, at] = slab_ref[:, at] - dot(left, depth_ref[:, at])


def groups_of(panel):
    return sorted({piece[1] for piece in pieces_of(panel)})


def update(place, after, panel, far, later, sides, factors, slab, target, pieces, grams, past, carry):
    rows, columns = slab.shape[0], slab.shape[1] // 2
    steps = 4
    deep = rows // steps
    size = factors.shape[-1]
    strip = pl.BlockSpec((deep, columns), lambda j, place: (j, place[1] ^ far))
    fixed = lambda x: pl.BlockSpec(x.shape, lambda j, place: (0,) * len(x.shape), pipeline_mode=pl.Buffered(1))
    block = pl.BlockSpec((1, deep, LANES), lambda j, place: (panel, j, 0))
    factor = pl.BlockSpec((1, size, size), lambda j, place: (panel, 0, 0), pipeline_mode=pl.Buffered(1))
    constant = list(pieces) + list(grams) + list(past) + list(carry)
    outs, out_specs = [shape(*slab.shape)], [strip]
    if later:
        extra = shape(later * size, columns) if grams else jax.ShapeDtypeStruct((3 * size, columns), jnp.bfloat16)
        outs.append(extra)
        out_specs.append(pl.BlockSpec(extra.shape, lambda j, place: (0, 0)))
    outs.append(TOKEN)
    out_specs.append(pl.BlockSpec(TOKEN.shape, lambda j, place: (0, 0)))
    operands = [place, *after, factors, *constant, sides[0], sides[1], slab, *target]
    counts = dict(
        after=len(after), groups=len(pieces), grams=len(grams), past=len(past), carry=len(carry), target=len(target),
        extra=len(outs) - 2,
    )
    return pl.pallas_call(
        functools.partial(update_kernel, panel, counts),
        grid_spec=pltpu.PrefetchScalarGridSpec(
            num_scalar_prefetch=1,
            grid=(steps,),
            in_specs=[ANY] * len(after) + [factor] + [fixed(x) for x in constant] + [block, block, strip] + [ANY] * len(target),
            out_specs=out_specs,
            scratch_shapes=[pltpu.VMEM((3 * size, columns), jnp.bfloat16), pltpu.VMEM((size, columns), F32)],
        ),
        out_shape=outs,
        input_output_aliases={len(operands) - 1: 0} if panel or target else {},
        compiler_params=params(),
        cost_estimate=COST,
        name=f"update_{panel}" + "ab"[far],
    )(*operands)


def order_of(kind, bits):
    first, second = (0, 1) if kind == 0 else (1, 0)
    order = [first, 2, second] + list(range(3, bits)) if bits > 2 else [first, second]
    return order[:bits]


def swap(value, step):
    rows, cores = lax.axis_size("row"), lax.axis_size("col")
    bits = rows.bit_length() - 1
    pairs = [
        (row * cores + core, (row ^ (1 << order_of(core % 2, bits)[step])) * cores + core)
        for row in range(rows)
        for core in range(cores)
    ]
    return lax.ppermute(value, ("row", "col"), pairs)


def shift(value, step):
    count = lax.axis_size("col")
    return lax.ppermute(value, "col", [((target + step) % count, target) for target in range(count)])


def body(eigvecs, reflectors, factors):
    panels, _, width = reflectors.shape
    size = factors.shape[-1]
    others = size // width
    bits = lax.axis_size("row").bit_length() - 1
    slots = min(lax.axis_size("row"), eigvecs.shape[1] // LANES)
    cuts = slots.bit_length() - 1
    me, core = lax.axis_index("row"), lax.axis_index("col")
    own = [
        sum(((me >> bit) & 1) << (cuts - 1 - at) for at, bit in enumerate(order_of(kind, bits)[:cuts])) for kind in range(2)
    ]
    block = jnp.where(core % 2 == 0, own[0], own[1])
    place = jnp.stack([block, block >> (cuts - 1)]).astype(jnp.int32)

    parts = [reflectors] + [shift(reflectors, step) for step in range(1, others)]
    join = lambda some: some[0] if len(some) == 1 else jnp.concatenate(some, axis=2)
    sides = [join(parts[: others // 2]), join(parts[others // 2 :])]
    factor_rows = jnp.concatenate([factors] + [shift(factors, step) for step in range(1, others)], axis=1)
    factors = lax.dynamic_slice_in_dim(jnp.concatenate([factor_rows, factor_rows], axis=2), core * width, size, axis=2)

    after = [jnp.zeros(TOKEN.shape, F32)]
    state, grams, slab = {}, [], eigvecs
    past, carry = [[], []], [[], []]

    def kernel(function, name, ins, outs):
        nonlocal after
        *made, token = small_call(function, name, after, place, ins, outs)
        after = [token]
        return made

    for event in schedule(bits + cuts - 1, panels):
        if event[0] == "p":
            call = CALLS[int(event[1:])]
            after = after + ([factors] if event == "p1" else [])
            made, token = project(place, after, sides, call, eigvecs, grams if call == (GRAM_GROUP,) else [], slots)
            after = [token]
            for group, (keep, send) in zip(call, made):
                state[group] = [keep, swap(send, 0)]
        elif event == "g":
            rows, token = gram(place, after, reflectors, sides, slots)
            grams, after = [rows], [token]
        elif event[0] == "k":
            step, group = map(int, event[1:].split("."))
            held = state[group]
            wide, tall, _ = held[0].shape
            if step < cuts:
                keep, send = kernel(halve_kernel, f"halve{step}_{group}", held, [shape(wide // 2, tall, LANES)] * 2)
                state[group] = [keep, swap(send, step)]
            elif step <= bits:
                (total,) = kernel(add_kernel, f"sum{step}_{group}", held, [shape(*held[0].shape)])
                state[group] = [total, swap(total, step if step < bits else cuts - 1)]
            else:
                (block,) = kernel(join_kernel, f"join{step}_{group}", held, [shape(2 * wide, tall, LANES)])
                state[group] = [block, swap(block, cuts - 1 - (step - bits))]
        elif event[0] == "f":
            after = after + [state[int(event[2:])][1]]
        elif event == "x":
            wide = panels * (panels - 1) // 2 * size
            (rows,) = kernel(gram_rows_kernel, "gram_own", state[GRAM_GROUP], [shape(width, wide)])
            grams = [rows] + [shift(rows, step) for step in range(1, others)]
        else:
            panel, far = int(event[1]), "ab".index(event[2])
            later = panels - 1 - panel
            pieces = [state[group][far] for group in groups_of(panel)]
            source, target = (eigvecs, [slab] if far else []) if panel == 0 else (slab, [])
            slab, *extra, token = update(
                place, after, panel, far, later, sides, factors, source, target, pieces,
                grams if panel and later else [], past[far] if panel == 1 else [], carry[far],
            )
            (carry if panel else past)[far] = extra
            after = [token]
    return slab


def solution(mesh):
    in_specs = (P("row", "col"), P(None, "row", "col"), P(None, "col", None))
    out_specs = P("row", "col")
    return jax.shard_map(body, mesh=mesh, in_specs=in_specs, out_specs=out_specs, check_vma=False)
```

```python
import functools

import jax
import jax.numpy as jnp
from jax import lax
from jax.experimental import pallas as pl
from jax.experimental.pallas import tpu as pltpu
from jax.sharding import PartitionSpec as P

LANES = 128
SIZE = 2 * LANES
VMEM_LIMIT = 40 * 1024 * 1024
FIRST_LIMIT = 58 * 1024 * 1024
F32 = jnp.float32

GROUPS = (
    ((0, 0, 0, 128), (1, 0, 0, 128)),
    ((0, 1, 0, 128), (1, 1, 0, 128)),
    ((2, 0, 0, 128), (2, 1, 0, 128)),
    ((3, 0, 0, 128), (3, 1, 0, 128)),
)
GRAM_GROUP = 1
CALLS = ((0,), (1,), (2,), (3,))
UPDATES = ((0, 1), (2,), (3,))
ORDER = (
    ["p0", "g", "p1", "k1.0", "p2", "k2.0", "k1.1", "p3", "k2.1", "k3.0", "k1.2", "k1.3", "k3.1", "k4.0", "k2.2"]
    + ["k4.1", "k3.2", "k5.0", "k2.3", "k6.0", "k5.1", "k4.2", "k3.3", "k6.1", "k4.3", "k5.2", "k7.0", "k6.2", "k5.3"]
    + ["k7.1", "f.0", "k6.3", "k7.2", "f.1", "x", "k7.3", "u0", "f.2", "u1", "f.3", "u2"]
)


def schedule(steps):
    if steps == 7:
        return ORDER
    groups = range(len(GROUPS))
    order = ["p0", "g"] + [f"p{call}" for call in range(1, len(CALLS))]
    order += [f"k{step}.{group}" for step in range(1, steps + 1) for group in groups]
    return order + ["x"] + [f"u{update}" for update in range(len(UPDATES))]


def rows_of(chunk):
    return sum(last - first for _, _, first, last in chunk)


def pieces_of(panel):
    found = []
    for group, chunk in enumerate(GROUPS):
        row = 0
        for some, side, first, last in chunk:
            if some == panel:
                found.append((side * LANES + first, group, row, last - first))
            row += last - first
    return sorted(found)


def halves(value):
    high = value.astype(jnp.bfloat16)
    low = (value - high.astype(F32)).astype(jnp.bfloat16)
    return high, low


def left_depth(value):
    high, low = halves(value)
    return jnp.concatenate([high, low, high], axis=1)


def right_depth(value):
    high, low = halves(value)
    return jnp.concatenate([high, high, low], axis=0)


def dot(left, right):
    return jnp.dot(left, right, preferred_element_type=F32)


def shape(*dims):
    return jax.ShapeDtypeStruct(dims, F32)


TOKEN = shape(8, LANES)
ANY = pl.BlockSpec(memory_space=pl.ANY)
SMEM = pl.BlockSpec(memory_space=pltpu.SMEM)

COST = pl.CostEstimate(flops=1, bytes_accessed=1, transcendentals=0)


def params(limit=VMEM_LIMIT):
    return pltpu.CompilerParams(vmem_limit_bytes=limit)


def whole(array):
    rank = len(array.shape)
    return pl.BlockSpec(array.shape, lambda *at: (0,) * rank, pipeline_mode=pl.Buffered(1))


def small_call(kernel, name, after, place, ins, outs):
    def run(place_ref, *refs):
        refs = refs[len(after) :]
        kernel(place_ref, refs[: len(ins)], refs[len(ins) : -1])
        refs[-1][...] = jnp.zeros(TOKEN.shape, F32)

    return pl.pallas_call(
        run,
        in_specs=[SMEM] + [ANY] * len(after) + [pl.BlockSpec(memory_space=pltpu.VMEM)] * len(ins),
        out_shape=list(outs) + [TOKEN],
        compiler_params=params(),
        cost_estimate=COST,
        name=name,
    )(place, *after, *ins)


def project_kernel(steps, call, blocks, skip, grams, place, *refs):
    block_refs, slab_ref, refs = refs[skip : skip + len(blocks)], refs[skip + len(blocks)], refs[skip + len(blocks) + 1 :]
    gram_refs, outs, token_out, total = refs[:grams], refs[grams:-2], refs[-2], refs[-1]
    step = pl.program_id(0)
    turned = {block: ref[0].T for block, ref in zip(blocks, block_refs)}
    left = left_depth(
        jnp.concatenate([turned[panel, side][first:last] for group in call for panel, side, first, last in GROUPS[group]])
    )
    wide = slab_ref.shape[1] // 4
    for quarter in range(4):
        at = pl.ds(quarter * wide, wide)
        made = dot(left, right_depth(slab_ref[:, at]))

        @pl.when(step == 0)
        def _():
            total[:, at] = made

        @pl.when(step > 0)
        def _():
            total[:, at] += made

    @pl.when(step == steps - 1)
    def _():
        token_out[...] = jnp.zeros(TOKEN.shape, F32)
        half = outs[0].shape[0]
        above = 0
        for at, group in enumerate(call):
            tall = rows_of(GROUPS[group])
            for slot in range(2 * half):
                out = outs[2 * at + slot // half]
                lanes = pl.ds(pl.multiple_of((place[0] ^ slot) * LANES, LANES), LANES)
                out[slot % half, :tall] = total[pl.ds(above, tall), lanes]
                if gram_refs:
                    out[slot % half, tall:] = gram_refs[0][slot]
            above += tall


def project(place, after, sides, call, slab, grams, slots):
    rows, columns = slab.shape
    steps = 2
    deep = rows // steps
    above = sum(rows_of(GROUPS[group]) for group in call)
    halves_of = []
    for group in call:
        tall = rows_of(GROUPS[group]) + sum(x.shape[1] for x in grams)
        halves_of += [shape(slots // 2, tall, LANES)] * 2
    blocks = sorted({(panel, side) for group in call for panel, side, _, _ in GROUPS[group]})
    specs = [pl.BlockSpec((1, deep, LANES), lambda j, panel=panel: (panel, j, 0)) for panel, _ in blocks]
    strip = pl.BlockSpec((deep, columns), lambda j: (j, 0))
    out = pl.pallas_call(
        functools.partial(project_kernel, steps, call, blocks, len(after), len(grams)),
        grid=(steps,),
        in_specs=[SMEM] + [ANY] * len(after) + specs + [strip] + [whole(x) for x in grams],
        out_specs=[pl.BlockSpec(x.shape, lambda j: (0, 0, 0)) for x in halves_of]
        + [pl.BlockSpec(TOKEN.shape, lambda j: (0, 0))],
        scratch_shapes=[pltpu.VMEM((above, columns), F32)],
        out_shape=halves_of + [TOKEN],
        compiler_params=params(FIRST_LIMIT if call == CALLS[0] else VMEM_LIMIT),
        cost_estimate=COST,
        name="project_" + "".join(map(str, call)),
    )(place, *after, *[sides[side] for _, side in blocks], slab, *grams)
    return [(out[2 * at], out[2 * at + 1]) for at in range(len(call))], out[-1]


def gram_kernel(place, *refs):
    own_ref, side0_ref, side1_ref, out, token_out, rows_ref = refs[-6:]
    panels, _, width = own_ref.shape
    for other in range(panels - 1):
        left = jnp.concatenate([own_ref[panel].T for panel in range(other + 1, panels)])
        right = jnp.concatenate([side0_ref[other], side1_ref[other]], axis=1)
        made = dot(left_depth(left), right_depth(right))
        for row, panel in enumerate(range(other + 1, panels)):
            at = (panel * (panel - 1) // 2 + other) * SIZE
            rows_ref[:, pl.ds(at, SIZE)] = made[row * width : (row + 1) * width]
    slots = out.shape[0]
    tall = width // slots
    for slot in range(slots):
        rows = pl.ds(pl.multiple_of((place[0] ^ slot) * tall, tall), tall)
        for block in range(rows_ref.shape[1] // LANES):
            out[slot, pl.ds(block * tall, tall)] = rows_ref[rows, pl.ds(block * LANES, LANES)]
    token_out[...] = jnp.zeros(TOKEN.shape, F32)


def gram(place, after, reflectors, sides, slots):
    panels, _, width = reflectors.shape
    wide = panels * (panels - 1) // 2 * SIZE
    ins = [reflectors, *sides]
    return pl.pallas_call(
        gram_kernel,
        in_specs=[SMEM] + [ANY] * len(after) + [pl.BlockSpec(memory_space=pltpu.VMEM)] * 3,
        scratch_shapes=[pltpu.VMEM((width, wide), F32)],
        out_shape=[shape(slots, width // slots * (wide // LANES), LANES), TOKEN],
        compiler_params=params(),
        cost_estimate=COST,
        name="gram_rows",
    )(place, *after, *ins)


def gram_rows_kernel(place, ins, outs):
    (out,) = outs
    above = rows_of(GROUPS[GRAM_GROUP])
    half = ins[0].shape[0]
    tall = out.shape[0] // (2 * half)
    for slot in range(2 * half):
        rows = pl.ds(pl.multiple_of((place[0] ^ slot) * tall, tall), tall)
        for block in range(out.shape[1] // LANES):
            out[rows, pl.ds(block * LANES, LANES)] = ins[slot // half][slot % half, pl.ds(above + block * tall, tall)]


def halve_kernel(place, ins, outs):
    keep, got = ins
    half = outs[0].shape[0]
    outs[0][...] = keep[:half] + got[:half]
    outs[1][...] = keep[half:] + got[half:]


def add_kernel(place, ins, outs):
    outs[0][...] = ins[0][...] + ins[1][...]


def join_kernel(place, ins, outs):
    half = ins[0].shape[0]
    outs[0][:half] = ins[0][...]
    outs[0][half:] = ins[1][...]


def update_kernel(panels, parts, carried, left_over, skip, groups, place, *refs):
    count = len(panels)
    factor_ref, refs = refs[skip], refs[skip + 1 :]
    summed = {group: refs[2 * at : 2 * at + 2] for at, group in enumerate(groups)}
    refs = refs[2 * len(groups) :]
    gram_refs, refs = refs[:parts], refs[parts:]
    carry_ref, refs = (refs[0], refs[1:]) if carried else (None, refs)
    blocks, slab_ref, out_ref = refs[: 2 * count], refs[2 * count], refs[2 * count + 1]
    depth_ref, proj_ref = refs[-2:]
    depth = count * SIZE
    columns = slab_ref.shape[1]
    wide = columns // 4

    def gram_block(panel, other):
        at = pl.ds((panel * (panel - 1) // 2 + other) * SIZE, SIZE)
        width = gram_refs[0].shape[0]
        rows = [ref[:, at] for ref in gram_refs]
        return jnp.concatenate([pltpu.roll(part, step * width, 1) if step else part for step, part in enumerate(rows)])

    @pl.when(pl.program_id(0) == 0)
    def _():
        for row, panel in enumerate(panels):
            for at, group, first, tall in pieces_of(panel):
                half = summed[group][0].shape[0]
                for slot in range(2 * half):
                    lanes = pl.ds(pl.multiple_of((place[0] ^ slot) * LANES, LANES), LANES)
                    proj_ref[pl.ds(row * SIZE + at, tall), lanes] = summed[group][slot // half][
                        slot % half, pl.ds(first, tall)
                    ]
        factor = [left_depth(factor_ref[row]) for row in range(count)]
        later = [panels[-1] + 1 + more for more in range(left_over)]
        grams = {
            (panel, row): left_depth(gram_block(panel, panels[row]))
            for panel in list(panels) + later
            for row in range(count)
            if panels[row] < panel
        }
        for quarter in range(4):
            at = pl.ds(quarter * wide, wide)
            past = []

            def less(value, panel, sign):
                for row, weights in enumerate(past):
                    value = value + sign * dot(grams[panel, row], weights)
                return value

            for row in range(count):
                proj = proj_ref[pl.ds(row * SIZE, SIZE), at]
                if carried:
                    proj = proj - carry_ref[pl.ds(row * SIZE, SIZE), at]
                proj = less(proj, panels[row], -1.0)
                high, low = halves(dot(factor[row], right_depth(proj)))
                past.append(jnp.concatenate([high, high, low]))
                for copy, value in enumerate([high, high, low]):
                    depth_ref[pl.ds(copy * depth + row * SIZE, SIZE), at] = value
            for more, panel in enumerate(later):
                value = carry_ref[pl.ds((count + more) * SIZE, SIZE), at] if carried else jnp.zeros((SIZE, wide), F32)
                refs[2 * count + 2][pl.ds(more * SIZE, SIZE), at] = less(value, panel, 1.0)

    left = left_depth(jnp.concatenate([ref[0] for ref in blocks], axis=1))
    for quarter in range(4):
        at = pl.ds(quarter * wide, wide)
        out_ref[:, at] = slab_ref[:, at] - dot(left, depth_ref[:, at])


def update(place, after, panels, left_over, sides, factors, slab, state, grams, carry):
    rows, columns = slab.shape
    steps = 4
    deep = rows // steps
    first, count = panels[0], len(panels)
    size = factors.shape[-1]
    groups = sorted({piece[1] for panel in panels for piece in pieces_of(panel)})
    strip = pl.BlockSpec((deep, columns), lambda j: (j, 0))
    specs, blocks = [], []
    for panel in panels:
        for side in range(2):
            specs.append(pl.BlockSpec((1, deep, LANES), lambda j, panel=panel: (panel, j, 0)))
            blocks.append(sides[side])
    factor = pl.BlockSpec((count, size, size), lambda j: (first // count, 0, 0), pipeline_mode=pl.Buffered(1))
    grams = grams if left_over or count > 1 else []
    carries = [] if carry is None else [carry]
    constant = [x for group in groups for x in state[group]] + list(grams) + carries
    outs, out_specs = [shape(rows, columns)], [strip]
    if left_over:
        outs.append(shape(left_over * size, columns))
        out_specs.append(pl.BlockSpec(outs[1].shape, lambda j: (0, 0)))
    made = pl.pallas_call(
        functools.partial(update_kernel, panels, len(grams), len(carries), left_over, len(after), groups),
        grid=(steps,),
        in_specs=[SMEM] + [ANY] * len(after) + [factor] + [whole(x) for x in constant] + specs + [strip],
        out_specs=out_specs,
        scratch_shapes=[pltpu.VMEM((3 * count * size, columns), jnp.bfloat16), pltpu.VMEM((count * size, columns), F32)],
        out_shape=outs,
        compiler_params=params(),
        cost_estimate=COST,
        name="update_panels" + "".join(map(str, panels)),
    )(place, *after, factors, *constant, *blocks, slab)
    return made[0], made[1] if left_over else None


def order_of(kind, bits):
    first, second = (0, 1) if kind == 0 else (1, 0)
    order = [first, 2, second] + list(range(3, bits)) if bits > 2 else [first, second]
    return order[:bits]


def swap(value, step):
    rows, cores = lax.axis_size("row"), lax.axis_size("col")
    bits = rows.bit_length() - 1
    pairs = [
        (row * cores + core, (row ^ (1 << order_of(core % 2, bits)[step])) * cores + core)
        for row in range(rows)
        for core in range(cores)
    ]
    return lax.ppermute(value, ("row", "col"), pairs)


def shift(value, step):
    count = lax.axis_size("col")
    return lax.ppermute(value, "col", [((target + step) % count, target) for target in range(count)])


def body(eigvecs, reflectors, factors):
    panels, _, width = reflectors.shape
    size = factors.shape[-1]
    others = size // width
    bits = lax.axis_size("row").bit_length() - 1
    slots = min(lax.axis_size("row"), eigvecs.shape[1] // LANES)
    cuts = slots.bit_length() - 1
    me, core = lax.axis_index("row"), lax.axis_index("col")
    own = [
        sum(((me >> bit) & 1) << (cuts - 1 - at) for at, bit in enumerate(order_of(kind, bits)[:cuts])) for kind in range(2)
    ]
    place = jnp.stack([jnp.where(core % 2 == 0, own[0], own[1])]).astype(jnp.int32)

    parts = [reflectors] + [shift(reflectors, step) for step in range(1, others)]
    join = lambda some: some[0] if len(some) == 1 else jnp.concatenate(some, axis=2)
    sides = [join(parts[: others // 2]), join(parts[others // 2 :])]
    factor_rows = jnp.concatenate([factors] + [shift(factors, step) for step in range(1, others)], axis=1)
    factors = lax.dynamic_slice_in_dim(jnp.concatenate([factor_rows, factor_rows], axis=2), core * width, size, axis=2)

    after = [jnp.zeros(TOKEN.shape, F32)]
    state, grams, slab, carry = {}, [], eigvecs, None

    def kernel(function, name, ins, outs):
        nonlocal after
        *made, token = small_call(function, name, after, place, ins, outs)
        after = [token]
        return made

    for event in schedule(bits + cuts - 1):
        if event[0] == "p":
            call = CALLS[int(event[1:])]
            after = after + ([factors] if event == "p1" else [])
            made, token = project(place, after, sides, call, eigvecs, grams if call == (GRAM_GROUP,) else [], slots)
            after = [token]
            for group, (keep, send) in zip(call, made):
                state[group] = [keep, swap(send, 0)]
        elif event == "g":
            rows, token = gram(place, after, reflectors, sides, slots)
            grams, after = [rows], [token]
        elif event[0] == "k":
            step, group = map(int, event[1:].split("."))
            held = state[group]
            wide, tall, _ = held[0].shape
            if step < cuts:
                keep, send = kernel(halve_kernel, f"halve{step}_{group}", held, [shape(wide // 2, tall, LANES)] * 2)
                state[group] = [keep, swap(send, step)]
            elif step <= bits:
                (total,) = kernel(add_kernel, f"sum{step}_{group}", held, [shape(*held[0].shape)])
                state[group] = [total, swap(total, step if step < bits else cuts - 1)]
            else:
                (block,) = kernel(join_kernel, f"join{step}_{group}", held, [shape(2 * wide, tall, LANES)])
                state[group] = [block, swap(block, cuts - 1 - (step - bits))]
        elif event[0] == "f":
            after = after + [state[int(event[2:])][1]]
        elif event == "x":
            wide = panels * (panels - 1) // 2 * size
            (rows,) = kernel(gram_rows_kernel, "gram_own", state[GRAM_GROUP], [shape(width, wide)])
            grams = [rows] + [shift(rows, step) for step in range(1, others)]
        else:
            some = UPDATES[int(event[1:])]
            slab, carry = update(
                place, after, some, panels - 1 - some[-1], sides, factors, slab, state, grams, carry
            )
            after = [slab]
    return slab


def solution(mesh):
    in_specs = (P("row", "col"), P(None, "row", "col"), P(None, "col", None))
    out_specs = P("row", "col")
    return jax.shard_map(body, mesh=mesh, in_specs=in_specs, out_specs=out_specs, check_vma=False)
```

```python
import functools

import jax
import jax.numpy as jnp
from jax import lax
from jax.experimental import pallas as pl
from jax.experimental.pallas import tpu as pltpu
from jax.sharding import PartitionSpec as P

LANES = 128
SIZE = 2 * LANES
VMEM_LIMIT = 40 * 1024 * 1024
FIRST_LIMIT = 58 * 1024 * 1024
F32 = jnp.float32

GROUPS = (
    ((0, 0, 0, 128), (1, 0, 0, 128)),
    ((0, 1, 0, 128), (1, 1, 0, 128)),
    ((2, 0, 0, 128), (2, 1, 0, 128)),
    ((3, 0, 0, 128), (3, 1, 0, 128)),
)
GRAM_GROUP = 1
CALLS = ((0,), (1,), (2,), (3,))
UPDATES = ((0, 1), (2,), (3,))
ORDER = (
    ["p0", "g", "p1", "k1.0", "p2", "k2.0", "k1.1", "p3", "k1.2", "k2.1", "k3.0", "k3.1", "k2.2", "k1.3", "k4.0"]
    + ["k3.2", "k4.1", "k5.0", "k2.3", "k6.0", "k4.2", "k5.1", "k3.3", "k6.1", "k5.2", "k4.3", "k7.0", "k6.2", "k5.3"]
    + ["k7.1", "f.0", "k6.3", "k7.2", "k7.3", "f.1", "x", "u0", "f.2", "u1", "f.3", "u2"]
)


def schedule(steps):
    if steps == 7:
        return ORDER
    groups = range(len(GROUPS))
    order = ["p0", "g"] + [f"p{call}" for call in range(1, len(CALLS))]
    order += [f"k{step}.{group}" for step in range(1, steps + 1) for group in groups]
    return order + ["x"] + [f"u{update}" for update in range(len(UPDATES))]


def rows_of(chunk):
    return sum(last - first for _, _, first, last in chunk)


def pieces_of(panel):
    found = []
    for group, chunk in enumerate(GROUPS):
        row = 0
        for some, side, first, last in chunk:
            if some == panel:
                found.append((side * LANES + first, group, row, last - first))
            row += last - first
    return sorted(found)


def halves(value):
    high = value.astype(jnp.bfloat16)
    low = (value - high.astype(F32)).astype(jnp.bfloat16)
    return high, low


def left_depth(value):
    high, low = halves(value)
    return jnp.concatenate([high, low, high], axis=1)


def right_depth(value):
    high, low = halves(value)
    return jnp.concatenate([high, high, low], axis=0)


def dot(left, right):
    return jnp.dot(left, right, preferred_element_type=F32)


def shape(*dims):
    return jax.ShapeDtypeStruct(dims, F32)


TOKEN = shape(8, LANES)
ANY = pl.BlockSpec(memory_space=pl.ANY)
SMEM = pl.BlockSpec(memory_space=pltpu.SMEM)

COST = pl.CostEstimate(flops=10**10, bytes_accessed=100, transcendentals=0)


def params(limit=VMEM_LIMIT):
    return pltpu.CompilerParams(vmem_limit_bytes=limit)


def whole(array):
    rank = len(array.shape)
    return pl.BlockSpec(array.shape, lambda *at: (0,) * rank, pipeline_mode=pl.Buffered(1))


def small_call(kernel, name, after, place, ins, outs):
    def run(place_ref, *refs):
        refs = refs[len(after) :]
        kernel(place_ref, refs[: len(ins)], refs[len(ins) : -1])
        refs[-1][...] = jnp.zeros(TOKEN.shape, F32)

    return pl.pallas_call(
        run,
        in_specs=[SMEM] + [ANY] * len(after) + [pl.BlockSpec(memory_space=pltpu.VMEM)] * len(ins),
        out_shape=list(outs) + [TOKEN],
        compiler_params=params(),
        cost_estimate=COST,
        name=name,
    )(place, *after, *ins)


def project_kernel(steps, call, blocks, skip, grams, place, *refs):
    block_refs, slab_ref, refs = refs[skip : skip + len(blocks)], refs[skip + len(blocks)], refs[skip + len(blocks) + 1 :]
    gram_refs, outs, token_out, total = refs[:grams], refs[grams:-2], refs[-2], refs[-1]
    step = pl.program_id(0)
    turned = {block: ref[0].T for block, ref in zip(blocks, block_refs)}
    left = left_depth(
        jnp.concatenate([turned[panel, side][first:last] for group in call for panel, side, first, last in GROUPS[group]])
    )
    wide = slab_ref.shape[1] // 4
    for quarter in range(4):
        at = pl.ds(quarter * wide, wide)
        made = dot(left, right_depth(slab_ref[:, at]))

        @pl.when(step == 0)
        def _():
            total[:, at] = made

        @pl.when(step > 0)
        def _():
            total[:, at] += made

    @pl.when(step == steps - 1)
    def _():
        token_out[...] = jnp.zeros(TOKEN.shape, F32)
        half = outs[0].shape[0]
        above = 0
        for at, group in enumerate(call):
            tall = rows_of(GROUPS[group])
            for slot in range(2 * half):
                out = outs[2 * at + slot // half]
                lanes = pl.ds(pl.multiple_of((place[0] ^ slot) * LANES, LANES), LANES)
                out[slot % half, :tall] = total[pl.ds(above, tall), lanes]
                if gram_refs:
                    out[slot % half, tall:] = gram_refs[0][slot]
            above += tall


def project(place, after, sides, call, slab, grams, slots):
    rows, columns = slab.shape
    steps = 2
    deep = rows // steps
    above = sum(rows_of(GROUPS[group]) for group in call)
    halves_of = []
    for group in call:
        tall = rows_of(GROUPS[group]) + sum(x.shape[1] for x in grams)
        halves_of += [shape(slots // 2, tall, LANES)] * 2
    blocks = sorted({(panel, side) for group in call for panel, side, _, _ in GROUPS[group]})
    specs = [pl.BlockSpec((1, deep, LANES), lambda j, panel=panel: (panel, j, 0)) for panel, _ in blocks]
    strip = pl.BlockSpec((deep, columns), lambda j: (j, 0))
    out = pl.pallas_call(
        functools.partial(project_kernel, steps, call, blocks, len(after), len(grams)),
        grid=(steps,),
        in_specs=[SMEM] + [ANY] * len(after) + specs + [strip] + [whole(x) for x in grams],
        out_specs=[pl.BlockSpec(x.shape, lambda j: (0, 0, 0)) for x in halves_of]
        + [pl.BlockSpec(TOKEN.shape, lambda j: (0, 0))],
        scratch_shapes=[pltpu.VMEM((above, columns), F32)],
        out_shape=halves_of + [TOKEN],
        compiler_params=params(FIRST_LIMIT if call == CALLS[0] else VMEM_LIMIT),
        cost_estimate=COST,
        name="project_" + "".join(map(str, call)),
    )(place, *after, *[sides[side] for _, side in blocks], slab, *grams)
    return [(out[2 * at], out[2 * at + 1]) for at in range(len(call))], out[-1]


def gram_kernel(place, *refs):
    own_ref, side0_ref, side1_ref, out, token_out, rows_ref = refs[-6:]
    panels, _, width = own_ref.shape
    for other in range(panels - 1):
        left = jnp.concatenate([own_ref[panel].T for panel in range(other + 1, panels)])
        right = jnp.concatenate([side0_ref[other], side1_ref[other]], axis=1)
        made = dot(left_depth(left), right_depth(right))
        for row, panel in enumerate(range(other + 1, panels)):
            at = (panel * (panel - 1) // 2 + other) * SIZE
            rows_ref[:, pl.ds(at, SIZE)] = made[row * width : (row + 1) * width]
    slots = out.shape[0]
    tall = width // slots
    for slot in range(slots):
        rows = pl.ds(pl.multiple_of((place[0] ^ slot) * tall, tall), tall)
        for block in range(rows_ref.shape[1] // LANES):
            out[slot, pl.ds(block * tall, tall)] = rows_ref[rows, pl.ds(block * LANES, LANES)]
    token_out[...] = jnp.zeros(TOKEN.shape, F32)


def gram(place, after, reflectors, sides, slots):
    panels, _, width = reflectors.shape
    wide = panels * (panels - 1) // 2 * SIZE
    ins = [reflectors, *sides]
    return pl.pallas_call(
        gram_kernel,
        in_specs=[SMEM] + [ANY] * len(after) + [pl.BlockSpec(memory_space=pltpu.VMEM)] * 3,
        scratch_shapes=[pltpu.VMEM((width, wide), F32)],
        out_shape=[shape(slots, width // slots * (wide // LANES), LANES), TOKEN],
        compiler_params=params(),
        cost_estimate=COST,
        name="gram_rows",
    )(place, *after, *ins)


def gram_rows_kernel(place, ins, outs):
    (out,) = outs
    above = rows_of(GROUPS[GRAM_GROUP])
    half = ins[0].shape[0]
    tall = out.shape[0] // (2 * half)
    for slot in range(2 * half):
        rows = pl.ds(pl.multiple_of((place[0] ^ slot) * tall, tall), tall)
        for block in range(out.shape[1] // LANES):
            out[rows, pl.ds(block * LANES, LANES)] = ins[slot // half][slot % half, pl.ds(above + block * tall, tall)]


def halve_kernel(place, ins, outs):
    keep, got = ins
    half = outs[0].shape[0]
    outs[0][...] = keep[:half] + got[:half]
    outs[1][...] = keep[half:] + got[half:]


def add_kernel(place, ins, outs):
    outs[0][...] = ins[0][...] + ins[1][...]


def join_kernel(place, ins, outs):
    half = ins[0].shape[0]
    outs[0][:half] = ins[0][...]
    outs[0][half:] = ins[1][...]


def update_kernel(panels, parts, carried, left_over, skip, groups, place, *refs):
    count = len(panels)
    factor_ref, refs = refs[skip], refs[skip + 1 :]
    summed = {group: refs[2 * at : 2 * at + 2] for at, group in enumerate(groups)}
    refs = refs[2 * len(groups) :]
    gram_refs, refs = refs[:parts], refs[parts:]
    carry_ref, refs = (refs[0], refs[1:]) if carried else (None, refs)
    blocks, slab_ref, out_ref = refs[: 2 * count], refs[2 * count], refs[2 * count + 1]
    depth_ref, proj_ref = refs[-2:]
    depth = count * SIZE
    columns = slab_ref.shape[1]
    wide = columns // 4

    def gram_block(panel, other):
        at = pl.ds((panel * (panel - 1) // 2 + other) * SIZE, SIZE)
        width = gram_refs[0].shape[0]
        rows = [ref[:, at] for ref in gram_refs]
        return jnp.concatenate([pltpu.roll(part, step * width, 1) if step else part for step, part in enumerate(rows)])

    @pl.when(pl.program_id(0) == 0)
    def _():
        for row, panel in enumerate(panels):
            for at, group, first, tall in pieces_of(panel):
                half = summed[group][0].shape[0]
                for slot in range(2 * half):
                    lanes = pl.ds(pl.multiple_of((place[0] ^ slot) * LANES, LANES), LANES)
                    proj_ref[pl.ds(row * SIZE + at, tall), lanes] = summed[group][slot // half][
                        slot % half, pl.ds(first, tall)
                    ]
        factor = [left_depth(factor_ref[row]) for row in range(count)]
        later = [panels[-1] + 1 + more for more in range(left_over)]
        grams = {
            (panel, row): left_depth(gram_block(panel, panels[row]))
            for panel in list(panels) + later
            for row in range(count)
            if panels[row] < panel
        }
        for quarter in range(4):
            at = pl.ds(quarter * wide, wide)
            past = []

            def less(value, panel, sign):
                for row, weights in enumerate(past):
                    value = value + sign * dot(grams[panel, row], weights)
                return value

            for row in range(count):
                proj = proj_ref[pl.ds(row * SIZE, SIZE), at]
                if carried:
                    proj = proj - carry_ref[pl.ds(row * SIZE, SIZE), at]
                proj = less(proj, panels[row], -1.0)
                high, low = halves(dot(factor[row], right_depth(proj)))
                past.append(jnp.concatenate([high, high, low]))
                for copy, value in enumerate([high, high, low]):
                    depth_ref[pl.ds(copy * depth + row * SIZE, SIZE), at] = value
            for more, panel in enumerate(later):
                value = carry_ref[pl.ds((count + more) * SIZE, SIZE), at] if carried else jnp.zeros((SIZE, wide), F32)
                refs[2 * count + 2][pl.ds(more * SIZE, SIZE), at] = less(value, panel, 1.0)

    left = left_depth(jnp.concatenate([ref[0] for ref in blocks], axis=1))
    for quarter in range(4):
        at = pl.ds(quarter * wide, wide)
        out_ref[:, at] = slab_ref[:, at] - dot(left, depth_ref[:, at])


def update(place, after, panels, left_over, sides, factors, slab, state, grams, carry):
    rows, columns = slab.shape
    steps = 4 if len(panels) > 1 else 2
    deep = rows // steps
    first, count = panels[0], len(panels)
    size = factors.shape[-1]
    groups = sorted({piece[1] for panel in panels for piece in pieces_of(panel)})
    strip = pl.BlockSpec((deep, columns), lambda j: (j, 0))
    specs, blocks = [], []
    for panel in panels:
        for side in range(2):
            specs.append(pl.BlockSpec((1, deep, LANES), lambda j, panel=panel: (panel, j, 0)))
            blocks.append(sides[side])
    factor = pl.BlockSpec((count, size, size), lambda j: (first // count, 0, 0), pipeline_mode=pl.Buffered(1))
    grams = grams if left_over or count > 1 else []
    carries = [] if carry is None else [carry]
    constant = [x for group in groups for x in state[group]] + list(grams) + carries
    outs, out_specs = [shape(rows, columns)], [strip]
    if left_over:
        outs.append(shape(left_over * size, columns))
        out_specs.append(pl.BlockSpec(outs[1].shape, lambda j: (0, 0)))
    made = pl.pallas_call(
        functools.partial(update_kernel, panels, len(grams), len(carries), left_over, len(after), groups),
        grid=(steps,),
        in_specs=[SMEM] + [ANY] * len(after) + [factor] + [whole(x) for x in constant] + specs + [strip],
        out_specs=out_specs,
        scratch_shapes=[pltpu.VMEM((3 * count * size, columns), jnp.bfloat16), pltpu.VMEM((count * size, columns), F32)],
        out_shape=outs,
        compiler_params=params(),
        cost_estimate=COST,
        name="update_panels" + "".join(map(str, panels)),
    )(place, *after, factors, *constant, *blocks, slab)
    return made[0], made[1] if left_over else None


def order_of(kind, bits):
    first, second = (0, 1) if kind == 0 else (1, 0)
    order = [first, 2, second] + list(range(3, bits)) if bits > 2 else [first, second]
    return order[:bits]


def swap(value, step):
    rows, cores = lax.axis_size("row"), lax.axis_size("col")
    bits = rows.bit_length() - 1
    pairs = [
        (row * cores + core, (row ^ (1 << order_of(core % 2, bits)[step])) * cores + core)
        for row in range(rows)
        for core in range(cores)
    ]
    return lax.ppermute(value, ("row", "col"), pairs)


def shift(value, step):
    count = lax.axis_size("col")
    return lax.ppermute(value, "col", [((target + step) % count, target) for target in range(count)])


def body(eigvecs, reflectors, factors):
    panels, _, width = reflectors.shape
    size = factors.shape[-1]
    others = size // width
    bits = lax.axis_size("row").bit_length() - 1
    slots = min(lax.axis_size("row"), eigvecs.shape[1] // LANES)
    cuts = slots.bit_length() - 1
    me, core = lax.axis_index("row"), lax.axis_index("col")
    own = [
        sum(((me >> bit) & 1) << (cuts - 1 - at) for at, bit in enumerate(order_of(kind, bits)[:cuts])) for kind in range(2)
    ]
    place = jnp.stack([jnp.where(core % 2 == 0, own[0], own[1])]).astype(jnp.int32)

    parts = [reflectors] + [shift(reflectors, step) for step in range(1, others)]
    join = lambda some: some[0] if len(some) == 1 else jnp.concatenate(some, axis=2)
    sides = [join(parts[: others // 2]), join(parts[others // 2 :])]
    factor_rows = jnp.concatenate([factors] + [shift(factors, step) for step in range(1, others)], axis=1)
    factors = lax.dynamic_slice_in_dim(jnp.concatenate([factor_rows, factor_rows], axis=2), core * width, size, axis=2)

    after = [jnp.zeros(TOKEN.shape, F32)]
    state, grams, slab, carry = {}, [], eigvecs, None

    def kernel(function, name, ins, outs):
        nonlocal after
        *made, token = small_call(function, name, after, place, ins, outs)
        after = [token]
        return made

    for event in schedule(bits + cuts - 1):
        if event[0] == "p":
            call = CALLS[int(event[1:])]
            after = after + ([factors] if event == "p1" else [])
            made, token = project(place, after, sides, call, eigvecs, grams if call == (GRAM_GROUP,) else [], slots)
            after = [token]
            for group, (keep, send) in zip(call, made):
                state[group] = [keep, swap(send, 0)]
        elif event == "g":
            rows, token = gram(place, after, reflectors, sides, slots)
            grams, after = [rows], [token]
        elif event[0] == "k":
            step, group = map(int, event[1:].split("."))
            held = state[group]
            wide, tall, _ = held[0].shape
            if step < cuts:
                keep, send = kernel(halve_kernel, f"halve{step}_{group}", held, [shape(wide // 2, tall, LANES)] * 2)
                state[group] = [keep, swap(send, step)]
            elif step <= bits:
                (total,) = kernel(add_kernel, f"sum{step}_{group}", held, [shape(*held[0].shape)])
                state[group] = [total, swap(total, step if step < bits else cuts - 1)]
            else:
                (block,) = kernel(join_kernel, f"join{step}_{group}", held, [shape(2 * wide, tall, LANES)])
                state[group] = [block, swap(block, cuts - 1 - (step - bits))]
        elif event[0] == "f":
            after = after + [state[int(event[2:])][1]]
        elif event == "x":
            wide = panels * (panels - 1) // 2 * size
            (rows,) = kernel(gram_rows_kernel, "gram_own", state[GRAM_GROUP], [shape(width, wide)])
            grams = [rows] + [shift(rows, step) for step in range(1, others)]
        else:
            some = UPDATES[int(event[1:])]
            slab, carry = update(
                place, after, some, panels - 1 - some[-1], sides, factors, slab, state, grams, carry
            )
            after = [slab]
    return slab


def solution(mesh):
    in_specs = (P("row", "col"), P(None, "row", "col"), P(None, "col", None))
    out_specs = P("row", "col")
    return jax.shard_map(body, mesh=mesh, in_specs=in_specs, out_specs=out_specs, check_vma=False)
```

```python
import functools

import jax
import jax.numpy as jnp
from jax import lax
from jax.experimental import pallas as pl
from jax.experimental.pallas import tpu as pltpu
from jax.sharding import PartitionSpec as P

LANES = 128
SIZE = 2 * LANES
VMEM_LIMIT = 40 * 1024 * 1024
FIRST_LIMIT = 58 * 1024 * 1024
F32 = jnp.float32

GROUPS = (
    ((0, 0, 0, 128), (1, 0, 0, 128)),
    ((0, 1, 0, 128), (1, 1, 0, 128)),
    ((2, 0, 0, 128), (2, 1, 0, 128)),
    ((3, 0, 0, 128), (3, 1, 0, 128)),
)
GRAM_GROUP = 1
CALLS = ((0,), (1,), (2,), (3,))
UPDATES = ((0, 1), (2,), (3,))
ORDER = (
    ["p0", "g", "p1", "k1.0", "p2", "k2.0", "p3", "k1.1", "k3.0", "k1.2", "k2.1", "k1.3", "k4.0", "k3.1", "k2.2"]
    + ["k5.0", "k3.2", "k4.1", "k6.0", "k2.3", "k5.1", "k4.2", "k3.3", "k6.1", "k5.2", "k4.3", "k7.0", "k6.2", "k5.3"]
    + ["k7.1", "f.0", "k6.3", "k7.2", "k7.3", "f.1", "x", "u0", "f.2", "u1", "f.3", "u2"]
)


def schedule(steps):
    if steps == 7:
        return ORDER
    groups = range(len(GROUPS))
    order = ["p0", "g"] + [f"p{call}" for call in range(1, len(CALLS))]
    order += [f"k{step}.{group}" for step in range(1, steps + 1) for group in groups]
    return order + ["x"] + [f"u{update}" for update in range(len(UPDATES))]


def rows_of(chunk):
    return sum(last - first for _, _, first, last in chunk)


def pieces_of(panel):
    found = []
    for group, chunk in enumerate(GROUPS):
        row = 0
        for some, side, first, last in chunk:
            if some == panel:
                found.append((side * LANES + first, group, row, last - first))
            row += last - first
    return sorted(found)


def halves(value):
    high = value.astype(jnp.bfloat16)
    low = (value - high.astype(F32)).astype(jnp.bfloat16)
    return high, low


def left_depth(value):
    high, low = halves(value)
    return jnp.concatenate([high, low, high], axis=1)


def right_depth(value):
    high, low = halves(value)
    return jnp.concatenate([high, high, low], axis=0)


def dot(left, right):
    return jnp.dot(left, right, preferred_element_type=F32)


def shape(*dims):
    return jax.ShapeDtypeStruct(dims, F32)


TOKEN = shape(8, LANES)
ANY = pl.BlockSpec(memory_space=pl.ANY)
SMEM = pl.BlockSpec(memory_space=pltpu.SMEM)

COST = pl.CostEstimate(flops=10**10, bytes_accessed=100, transcendentals=0)


def params(limit=VMEM_LIMIT):
    return pltpu.CompilerParams(vmem_limit_bytes=limit)


def whole(array):
    rank = len(array.shape)
    return pl.BlockSpec(array.shape, lambda *at: (0,) * rank, pipeline_mode=pl.Buffered(1))


def small_call(kernel, name, after, place, ins, outs):
    def run(place_ref, *refs):
        refs = refs[len(after) :]
        kernel(place_ref, refs[: len(ins)], refs[len(ins) : -1])
        refs[-1][...] = jnp.zeros(TOKEN.shape, F32)

    return pl.pallas_call(
        run,
        in_specs=[SMEM] + [ANY] * len(after) + [pl.BlockSpec(memory_space=pltpu.VMEM)] * len(ins),
        out_shape=list(outs) + [TOKEN],
        compiler_params=params(),
        cost_estimate=COST,
        name=name,
    )(place, *after, *ins)


def project_kernel(steps, call, blocks, skip, grams, place, *refs):
    block_refs, slab_ref, refs = refs[skip : skip + len(blocks)], refs[skip + len(blocks)], refs[skip + len(blocks) + 1 :]
    gram_refs, outs, token_out, total = refs[:grams], refs[grams:-2], refs[-2], refs[-1]
    step = pl.program_id(0)
    turned = {block: ref[0].T for block, ref in zip(blocks, block_refs)}
    left = left_depth(
        jnp.concatenate([turned[panel, side][first:last] for group in call for panel, side, first, last in GROUPS[group]])
    )
    wide = slab_ref.shape[1] // 4
    for quarter in range(4):
        at = pl.ds(quarter * wide, wide)
        made = dot(left, right_depth(slab_ref[:, at]))

        @pl.when(step == 0)
        def _():
            total[:, at] = made

        @pl.when(step > 0)
        def _():
            total[:, at] += made

    @pl.when(step == steps - 1)
    def _():
        token_out[...] = jnp.zeros(TOKEN.shape, F32)
        half = outs[0].shape[0]
        above = 0
        for at, group in enumerate(call):
            tall = rows_of(GROUPS[group])
            for slot in range(2 * half):
                out = outs[2 * at + slot // half]
                lanes = pl.ds(pl.multiple_of((place[0] ^ slot) * LANES, LANES), LANES)
                out[slot % half, :tall] = total[pl.ds(above, tall), lanes]
                if gram_refs:
                    out[slot % half, tall:] = gram_refs[0][slot]
            above += tall


def project(place, after, sides, call, slab, grams, slots):
    rows, columns = slab.shape
    steps = 2
    deep = rows // steps
    above = sum(rows_of(GROUPS[group]) for group in call)
    halves_of = []
    for group in call:
        tall = rows_of(GROUPS[group]) + sum(x.shape[1] for x in grams)
        halves_of += [shape(slots // 2, tall, LANES)] * 2
    blocks = sorted({(panel, side) for group in call for panel, side, _, _ in GROUPS[group]})
    specs = [pl.BlockSpec((1, deep, LANES), lambda j, panel=panel: (panel, j, 0)) for panel, _ in blocks]
    strip = pl.BlockSpec((deep, columns), lambda j: (j, 0))
    out = pl.pallas_call(
        functools.partial(project_kernel, steps, call, blocks, len(after), len(grams)),
        grid=(steps,),
        in_specs=[SMEM] + [ANY] * len(after) + specs + [strip] + [whole(x) for x in grams],
        out_specs=[pl.BlockSpec(x.shape, lambda j: (0, 0, 0)) for x in halves_of]
        + [pl.BlockSpec(TOKEN.shape, lambda j: (0, 0))],
        scratch_shapes=[pltpu.VMEM((above, columns), F32)],
        out_shape=halves_of + [TOKEN],
        compiler_params=params(FIRST_LIMIT if call == CALLS[0] else VMEM_LIMIT),
        cost_estimate=COST,
        name="project_" + "".join(map(str, call)),
    )(place, *after, *[sides[side] for _, side in blocks], slab, *grams)
    return [(out[2 * at], out[2 * at + 1]) for at in range(len(call))], out[-1]


def gram_kernel(place, *refs):
    own_ref, side0_ref, side1_ref, out, token_out, rows_ref = refs[-6:]
    panels, _, width = own_ref.shape
    for other in range(panels - 1):
        left = jnp.concatenate([own_ref[panel].T for panel in range(other + 1, panels)])
        right = jnp.concatenate([side0_ref[other], side1_ref[other]], axis=1)
        made = dot(left_depth(left), right_depth(right))
        for row, panel in enumerate(range(other + 1, panels)):
            at = (panel * (panel - 1) // 2 + other) * SIZE
            rows_ref[:, pl.ds(at, SIZE)] = made[row * width : (row + 1) * width]
    slots = out.shape[0]
    tall = width // slots
    for slot in range(slots):
        rows = pl.ds(pl.multiple_of((place[0] ^ slot) * tall, tall), tall)
        for block in range(rows_ref.shape[1] // LANES):
            out[slot, pl.ds(block * tall, tall)] = rows_ref[rows, pl.ds(block * LANES, LANES)]
    token_out[...] = jnp.zeros(TOKEN.shape, F32)


def gram(place, after, reflectors, sides, slots):
    panels, _, width = reflectors.shape
    wide = panels * (panels - 1) // 2 * SIZE
    ins = [reflectors, *sides]
    return pl.pallas_call(
        gram_kernel,
        in_specs=[SMEM] + [ANY] * len(after) + [pl.BlockSpec(memory_space=pltpu.VMEM)] * 3,
        scratch_shapes=[pltpu.VMEM((width, wide), F32)],
        out_shape=[shape(slots, width // slots * (wide // LANES), LANES), TOKEN],
        compiler_params=params(),
        cost_estimate=COST,
        name="gram_rows",
    )(place, *after, *ins)


def gram_rows_kernel(place, ins, outs):
    (out,) = outs
    above = rows_of(GROUPS[GRAM_GROUP])
    half = ins[0].shape[0]
    tall = out.shape[0] // (2 * half)
    for slot in range(2 * half):
        rows = pl.ds(pl.multiple_of((place[0] ^ slot) * tall, tall), tall)
        for block in range(out.shape[1] // LANES):
            out[rows, pl.ds(block * LANES, LANES)] = ins[slot // half][slot % half, pl.ds(above + block * tall, tall)]


def halve_kernel(place, ins, outs):
    keep, got = ins
    half = outs[0].shape[0]
    outs[0][...] = keep[:half] + got[:half]
    outs[1][...] = keep[half:] + got[half:]


def add_kernel(place, ins, outs):
    outs[0][...] = ins[0][...] + ins[1][...]


def join_kernel(place, ins, outs):
    half = ins[0].shape[0]
    outs[0][:half] = ins[0][...]
    outs[0][half:] = ins[1][...]


def update_kernel(panels, parts, carried, left_over, skip, groups, place, *refs):
    count = len(panels)
    factor_ref, refs = refs[skip], refs[skip + 1 :]
    summed = {group: refs[2 * at : 2 * at + 2] for at, group in enumerate(groups)}
    refs = refs[2 * len(groups) :]
    gram_refs, refs = refs[:parts], refs[parts:]
    carry_ref, refs = (refs[0], refs[1:]) if carried else (None, refs)
    blocks, slab_ref, out_ref = refs[: 2 * count], refs[2 * count], refs[2 * count + 1]
    depth_ref, proj_ref = refs[-2:]
    depth = count * SIZE
    columns = slab_ref.shape[1]
    wide = columns // 4

    def gram_block(panel, other):
        at = pl.ds((panel * (panel - 1) // 2 + other) * SIZE, SIZE)
        width = gram_refs[0].shape[0]
        rows = [ref[:, at] for ref in gram_refs]
        return jnp.concatenate([pltpu.roll(part, step * width, 1) if step else part for step, part in enumerate(rows)])

    @pl.when(pl.program_id(0) == 0)
    def _():
        for row, panel in enumerate(panels):
            for at, group, first, tall in pieces_of(panel):
                half = summed[group][0].shape[0]
                for slot in range(2 * half):
                    lanes = pl.ds(pl.multiple_of((place[0] ^ slot) * LANES, LANES), LANES)
                    proj_ref[pl.ds(row * SIZE + at, tall), lanes] = summed[group][slot // half][
                        slot % half, pl.ds(first, tall)
                    ]
        factor = [left_depth(factor_ref[row]) for row in range(count)]
        later = [panels[-1] + 1 + more for more in range(left_over)]
        ahead = list(panels) + later
        grams = [
            left_depth(jnp.concatenate([gram_block(panel, panels[row]) for panel in ahead[row + 1 :]]))
            if ahead[row + 1 :]
            else None
            for row in range(count)
        ]
        for quarter in range(4):
            at = pl.ds(quarter * wide, wide)
            taken = [None] * len(ahead)
            if carried:
                taken = [carry_ref[pl.ds(row * SIZE, SIZE), at] for row in range(len(ahead))]
            for row in range(count):
                proj = proj_ref[pl.ds(row * SIZE, SIZE), at]
                if taken[row] is not None:
                    proj = proj - taken[row]
                high, low = halves(dot(factor[row], right_depth(proj)))
                weights = jnp.concatenate([high, high, low])
                for copy, value in enumerate([high, high, low]):
                    depth_ref[pl.ds(copy * depth + row * SIZE, SIZE), at] = value
                if grams[row] is not None:
                    made = dot(grams[row], weights)
                    for more in range(row + 1, len(ahead)):
                        term = made[(more - row - 1) * SIZE : (more - row) * SIZE]
                        taken[more] = term if taken[more] is None else taken[more] + term
            for more in range(left_over):
                refs[2 * count + 2][pl.ds(more * SIZE, SIZE), at] = taken[count + more]

    left = left_depth(jnp.concatenate([ref[0] for ref in blocks], axis=1))
    for quarter in range(4):
        at = pl.ds(quarter * wide, wide)
        out_ref[:, at] = slab_ref[:, at] - dot(left, depth_ref[:, at])


def update(place, after, panels, left_over, sides, factors, slab, state, grams, carry):
    rows, columns = slab.shape
    steps = 2
    deep = rows // steps
    first, count = panels[0], len(panels)
    size = factors.shape[-1]
    groups = sorted({piece[1] for panel in panels for piece in pieces_of(panel)})
    strip = pl.BlockSpec((deep, columns), lambda j: (j, 0))
    specs, blocks = [], []
    for panel in panels:
        for side in range(2):
            specs.append(pl.BlockSpec((1, deep, LANES), lambda j, panel=panel: (panel, j, 0)))
            blocks.append(sides[side])
    factor = pl.BlockSpec((count, size, size), lambda j: (first // count, 0, 0), pipeline_mode=pl.Buffered(1))
    grams = grams if left_over or count > 1 else []
    carries = [] if carry is None else [carry]
    constant = [x for group in groups for x in state[group]] + list(grams) + carries
    outs, out_specs = [shape(rows, columns)], [strip]
    if left_over:
        outs.append(shape(left_over * size, columns))
        out_specs.append(pl.BlockSpec(outs[1].shape, lambda j: (0, 0)))
    made = pl.pallas_call(
        functools.partial(update_kernel, panels, len(grams), len(carries), left_over, len(after), groups),
        grid=(steps,),
        in_specs=[SMEM] + [ANY] * len(after) + [factor] + [whole(x) for x in constant] + specs + [strip],
        out_specs=out_specs,
        scratch_shapes=[pltpu.VMEM((3 * count * size, columns), jnp.bfloat16), pltpu.VMEM((count * size, columns), F32)],
        out_shape=outs,
        compiler_params=params(FIRST_LIMIT if count > 1 else VMEM_LIMIT),
        cost_estimate=COST,
        name="update_panels" + "".join(map(str, panels)),
    )(place, *after, factors, *constant, *blocks, slab)
    return made[0], made[1] if left_over else None


def order_of(kind, bits):
    first, second = (0, 1) if kind == 0 else (1, 0)
    order = [first, 2, second] + list(range(3, bits)) if bits > 2 else [first, second]
    return order[:bits]


def swap(value, step):
    rows, cores = lax.axis_size("row"), lax.axis_size("col")
    bits = rows.bit_length() - 1
    pairs = [
        (row * cores + core, (row ^ (1 << order_of(core % 2, bits)[step])) * cores + core)
        for row in range(rows)
        for core in range(cores)
    ]
    return lax.ppermute(value, ("row", "col"), pairs)


def shift(value, step):
    count = lax.axis_size("col")
    return lax.ppermute(value, "col", [((target + step) % count, target) for target in range(count)])


def body(eigvecs, reflectors, factors):
    panels, _, width = reflectors.shape
    size = factors.shape[-1]
    others = size // width
    bits = lax.axis_size("row").bit_length() - 1
    slots = min(lax.axis_size("row"), eigvecs.shape[1] // LANES)
    cuts = slots.bit_length() - 1
    me, core = lax.axis_index("row"), lax.axis_index("col")
    own = [
        sum(((me >> bit) & 1) << (cuts - 1 - at) for at, bit in enumerate(order_of(kind, bits)[:cuts])) for kind in range(2)
    ]
    place = jnp.stack([jnp.where(core % 2 == 0, own[0], own[1])]).astype(jnp.int32)

    parts = [reflectors] + [shift(reflectors, step) for step in range(1, others)]
    join = lambda some: some[0] if len(some) == 1 else jnp.concatenate(some, axis=2)
    sides = [join(parts[: others // 2]), join(parts[others // 2 :])]
    factor_rows = jnp.concatenate([factors] + [shift(factors, step) for step in range(1, others)], axis=1)
    factors = lax.dynamic_slice_in_dim(jnp.concatenate([factor_rows, factor_rows], axis=2), core * width, size, axis=2)

    after = [jnp.zeros(TOKEN.shape, F32)]
    state, grams, slab, carry = {}, [], eigvecs, None

    def kernel(function, name, ins, outs):
        nonlocal after
        *made, token = small_call(function, name, after, place, ins, outs)
        after = [token]
        return made

    for event in schedule(bits + cuts - 1):
        if event[0] == "p":
            call = CALLS[int(event[1:])]
            after = after + ([factors] if event == "p1" else [])
            made, token = project(place, after, sides, call, eigvecs, grams if call == (GRAM_GROUP,) else [], slots)
            after = [token]
            for group, (keep, send) in zip(call, made):
                state[group] = [keep, swap(send, 0)]
        elif event == "g":
            rows, token = gram(place, after, reflectors, sides, slots)
            grams, after = [rows], [token]
        elif event[0] == "k":
            step, group = map(int, event[1:].split("."))
            held = state[group]
            wide, tall, _ = held[0].shape
            if step < cuts:
                keep, send = kernel(halve_kernel, f"halve{step}_{group}", held, [shape(wide // 2, tall, LANES)] * 2)
                state[group] = [keep, swap(send, step)]
            elif step <= bits:
                (total,) = kernel(add_kernel, f"sum{step}_{group}", held, [shape(*held[0].shape)])
                state[group] = [total, swap(total, step if step < bits else cuts - 1)]
            else:
                (block,) = kernel(join_kernel, f"join{step}_{group}", held, [shape(2 * wide, tall, LANES)])
                state[group] = [block, swap(block, cuts - 1 - (step - bits))]
        elif event[0] == "f":
            after = after + [state[int(event[2:])][1]]
        elif event == "x":
            wide = panels * (panels - 1) // 2 * size
            (rows,) = kernel(gram_rows_kernel, "gram_own", state[GRAM_GROUP], [shape(width, wide)])
            grams = [rows] + [shift(rows, step) for step in range(1, others)]
        else:
            some = UPDATES[int(event[1:])]
            slab, carry = update(
                place, after, some, panels - 1 - some[-1], sides, factors, slab, state, grams, carry
            )
            after = [slab]
    return slab


def solution(mesh):
    in_specs = (P("row", "col"), P(None, "row", "col"), P(None, "col", None))
    out_specs = P("row", "col")
    return jax.shard_map(body, mesh=mesh, in_specs=in_specs, out_specs=out_specs, check_vma=False)
```

```python
import functools

import jax
import jax.numpy as jnp
from jax import lax
from jax.experimental import pallas as pl
from jax.experimental.pallas import tpu as pltpu
from jax.sharding import PartitionSpec as P

LANES = 128
SIZE = 2 * LANES
VMEM_LIMIT = 40 * 1024 * 1024
FIRST_LIMIT = 58 * 1024 * 1024
F32 = jnp.float32

GROUPS = (
    ((0, 0, 0, 128), (1, 0, 0, 128)),
    ((0, 1, 0, 128), (1, 1, 0, 128)),
    ((2, 0, 0, 128), (2, 1, 0, 128)),
    ((3, 0, 0, 128), (3, 1, 0, 128)),
)
GRAM_GROUP = 1
CALLS = ((0,), (1,), (2,), (3,))
UPDATES = ((0, 1), (2,), (3,))
ORDER = (
    ["p0", "g", "p1", "k1.0", "p2", "k2.0", "p3", "k1.1", "k3.0", "k1.2", "k2.1", "k1.3", "k4.0", "k3.1", "k2.2", "k5.0", "k3.2", "k4.1", "k6.0", "k2.3", "k5.1", "k4.2", "k3.3", "k6.1", "k5.2"]
    + ["k4.3", "k7.0", "k7.1", "k6.2", "k5.3", "f.0", "k6.3", "k7.2", "k7.3", "f.1", "x", "u0", "f.2", "u1", "f.3", "u2"]
)


def schedule(steps):
    if steps == 7:
        return ORDER
    groups = range(len(GROUPS))
    order = ["p0", "g"] + [f"p{call}" for call in range(1, len(CALLS))]
    order += [f"k{step}.{group}" for step in range(1, steps + 1) for group in groups]
    return order + ["x"] + [f"u{update}" for update in range(len(UPDATES))]


def rows_of(chunk):
    return sum(last - first for _, _, first, last in chunk)


def pieces_of(panel):
    found = []
    for group, chunk in enumerate(GROUPS):
        row = 0
        for some, side, first, last in chunk:
            if some == panel:
                found.append((side * LANES + first, group, row, last - first))
            row += last - first
    return sorted(found)


def halves(value):
    high = value.astype(jnp.bfloat16)
    low = (value - high.astype(F32)).astype(jnp.bfloat16)
    return high, low


def left_depth(value):
    high, low = halves(value)
    return jnp.concatenate([high, low, high], axis=1)


def right_depth(value):
    high, low = halves(value)
    return jnp.concatenate([high, high, low], axis=0)


def dot(left, right):
    return jnp.dot(left, right, preferred_element_type=F32)


def shape(*dims):
    return jax.ShapeDtypeStruct(dims, F32)


TOKEN = shape(8, LANES)
ANY = pl.BlockSpec(memory_space=pl.ANY)
SMEM = pl.BlockSpec(memory_space=pltpu.SMEM)

COST = pl.CostEstimate(flops=3*10**9, bytes_accessed=100, transcendentals=0)


def params(limit=VMEM_LIMIT):
    return pltpu.CompilerParams(vmem_limit_bytes=limit)


def whole(array):
    rank = len(array.shape)
    return pl.BlockSpec(array.shape, lambda *at: (0,) * rank, pipeline_mode=pl.Buffered(1))


def small_call(kernel, name, after, place, ins, outs):
    def run(place_ref, *refs):
        refs = refs[len(after) :]
        kernel(place_ref, refs[: len(ins)], refs[len(ins) : -1])
        refs[-1][...] = jnp.zeros(TOKEN.shape, F32)

    return pl.pallas_call(
        run,
        in_specs=[SMEM] + [ANY] * len(after) + [pl.BlockSpec(memory_space=pltpu.VMEM)] * len(ins),
        out_shape=list(outs) + [TOKEN],
        compiler_params=params(),
        cost_estimate=COST,
        name=name,
    )(place, *after, *ins)


def project_kernel(steps, call, blocks, skip, grams, place, *refs):
    block_refs, slab_ref, refs = refs[skip : skip + len(blocks)], refs[skip + len(blocks)], refs[skip + len(blocks) + 1 :]
    gram_refs, outs, token_out, total = refs[:grams], refs[grams:-2], refs[-2], refs[-1]
    step = pl.program_id(0)
    turned = {block: ref[0].T for block, ref in zip(blocks, block_refs)}
    left = left_depth(
        jnp.concatenate([turned[panel, side][first:last] for group in call for panel, side, first, last in GROUPS[group]])
    )
    wide = slab_ref.shape[1] // 4
    for quarter in range(4):
        at = pl.ds(quarter * wide, wide)
        made = dot(left, right_depth(slab_ref[:, at]))

        @pl.when(step == 0)
        def _():
            total[:, at] = made

        @pl.when(step > 0)
        def _():
            total[:, at] += made

    @pl.when(step == steps - 1)
    def _():
        token_out[...] = jnp.zeros(TOKEN.shape, F32)
        half = outs[0].shape[0]
        above = 0
        for at, group in enumerate(call):
            tall = rows_of(GROUPS[group])
            for slot in range(2 * half):
                out = outs[2 * at + slot // half]
                lanes = pl.ds(pl.multiple_of((place[0] ^ slot) * LANES, LANES), LANES)
                out[slot % half, :tall] = total[pl.ds(above, tall), lanes]
                if gram_refs:
                    out[slot % half, tall:] = gram_refs[0][slot]
            above += tall


def project(place, after, sides, call, slab, grams, slots):
    rows, columns = slab.shape
    steps = 2
    deep = rows // steps
    above = sum(rows_of(GROUPS[group]) for group in call)
    halves_of = []
    for group in call:
        tall = rows_of(GROUPS[group]) + sum(x.shape[1] for x in grams)
        halves_of += [shape(slots // 2, tall, LANES)] * 2
    blocks = sorted({(panel, side) for group in call for panel, side, _, _ in GROUPS[group]})
    specs = [pl.BlockSpec((1, deep, LANES), lambda j, panel=panel: (panel, j, 0)) for panel, _ in blocks]
    strip = pl.BlockSpec((deep, columns), lambda j: (j, 0))
    out = pl.pallas_call(
        functools.partial(project_kernel, steps, call, blocks, len(after), len(grams)),
        grid=(steps,),
        in_specs=[SMEM] + [ANY] * len(after) + specs + [strip] + [whole(x) for x in grams],
        out_specs=[pl.BlockSpec(x.shape, lambda j: (0, 0, 0)) for x in halves_of]
        + [pl.BlockSpec(TOKEN.shape, lambda j: (0, 0))],
        scratch_shapes=[pltpu.VMEM((above, columns), F32)],
        out_shape=halves_of + [TOKEN],
        compiler_params=params(FIRST_LIMIT if call == CALLS[0] else VMEM_LIMIT),
        cost_estimate=COST,
        name="project_" + "".join(map(str, call)),
    )(place, *after, *[sides[side] for _, side in blocks], slab, *grams)
    return [(out[2 * at], out[2 * at + 1]) for at in range(len(call))], out[-1]


def gram_kernel(place, *refs):
    own_ref, side0_ref, side1_ref, out, token_out, rows_ref = refs[-6:]
    panels, _, width = own_ref.shape
    for other in range(panels - 1):
        left = jnp.concatenate([own_ref[panel].T for panel in range(other + 1, panels)])
        right = jnp.concatenate([side0_ref[other], side1_ref[other]], axis=1)
        made = dot(left_depth(left), right_depth(right))
        for row, panel in enumerate(range(other + 1, panels)):
            at = (panel * (panel - 1) // 2 + other) * SIZE
            rows_ref[:, pl.ds(at, SIZE)] = made[row * width : (row + 1) * width]
    slots = out.shape[0]
    tall = width // slots
    for slot in range(slots):
        rows = pl.ds(pl.multiple_of((place[0] ^ slot) * tall, tall), tall)
        for block in range(rows_ref.shape[1] // LANES):
            out[slot, pl.ds(block * tall, tall)] = rows_ref[rows, pl.ds(block * LANES, LANES)]
    token_out[...] = jnp.zeros(TOKEN.shape, F32)


def gram(place, after, reflectors, sides, slots):
    panels, _, width = reflectors.shape
    wide = panels * (panels - 1) // 2 * SIZE
    ins = [reflectors, *sides]
    return pl.pallas_call(
        gram_kernel,
        in_specs=[SMEM] + [ANY] * len(after) + [pl.BlockSpec(memory_space=pltpu.VMEM)] * 3,
        scratch_shapes=[pltpu.VMEM((width, wide), F32)],
        out_shape=[shape(slots, width // slots * (wide // LANES), LANES), TOKEN],
        compiler_params=params(),
        cost_estimate=COST,
        name="gram_rows",
    )(place, *after, *ins)


def gram_rows_kernel(place, ins, outs):
    (out,) = outs
    above = rows_of(GROUPS[GRAM_GROUP])
    half = ins[0].shape[0]
    tall = out.shape[0] // (2 * half)
    for slot in range(2 * half):
        rows = pl.ds(pl.multiple_of((place[0] ^ slot) * tall, tall), tall)
        for block in range(out.shape[1] // LANES):
            out[rows, pl.ds(block * LANES, LANES)] = ins[slot // half][slot % half, pl.ds(above + block * tall, tall)]


def halve_kernel(place, ins, outs):
    keep, got = ins
    half = outs[0].shape[0]
    outs[0][...] = keep[:half] + got[:half]
    outs[1][...] = keep[half:] + got[half:]


def add_kernel(place, ins, outs):
    outs[0][...] = ins[0][...] + ins[1][...]


def join_kernel(place, ins, outs):
    half = ins[0].shape[0]
    outs[0][:half] = ins[0][...]
    outs[0][half:] = ins[1][...]


def update_kernel(panels, parts, carried, left_over, skip, groups, place, *refs):
    count = len(panels)
    factor_ref, refs = refs[skip], refs[skip + 1 :]
    summed = {group: refs[2 * at : 2 * at + 2] for at, group in enumerate(groups)}
    refs = refs[2 * len(groups) :]
    gram_refs, refs = refs[:parts], refs[parts:]
    carry_ref, refs = (refs[0], refs[1:]) if carried else (None, refs)
    blocks, slab_ref, out_ref = refs[: 2 * count], refs[2 * count], refs[2 * count + 1]
    depth_ref, proj_ref = refs[-2:]
    depth = count * SIZE
    columns = slab_ref.shape[1]
    wide = columns // 4

    def gram_block(panel, other):
        at = pl.ds((panel * (panel - 1) // 2 + other) * SIZE, SIZE)
        width = gram_refs[0].shape[0]
        rows = [ref[:, at] for ref in gram_refs]
        return jnp.concatenate([pltpu.roll(part, step * width, 1) if step else part for step, part in enumerate(rows)])

    @pl.when(pl.program_id(0) == 0)
    def _():
        for row, panel in enumerate(panels):
            for at, group, first, tall in pieces_of(panel):
                half = summed[group][0].shape[0]
                for slot in range(2 * half):
                    lanes = pl.ds(pl.multiple_of((place[0] ^ slot) * LANES, LANES), LANES)
                    proj_ref[pl.ds(row * SIZE + at, tall), lanes] = summed[group][slot // half][
                        slot % half, pl.ds(first, tall)
                    ]
        factor = [left_depth(factor_ref[row]) for row in range(count)]
        later = [panels[-1] + 1 + more for more in range(left_over)]
        grams = {
            (panel, row): left_depth(gram_block(panel, panels[row]))
            for panel in list(panels) + later
            for row in range(count)
            if panels[row] < panel
        }
        for quarter in range(4):
            at = pl.ds(quarter * wide, wide)
            past = []

            def less(value, panel, sign):
                for row, weights in enumerate(past):
                    value = value + sign * dot(grams[panel, row], weights)
                return value

            for row in range(count):
                proj = proj_ref[pl.ds(row * SIZE, SIZE), at]
                if carried:
                    proj = proj - carry_ref[pl.ds(row * SIZE, SIZE), at]
                proj = less(proj, panels[row], -1.0)
                high, low = halves(dot(factor[row], right_depth(proj)))
                past.append(jnp.concatenate([high, high, low]))
                for copy, value in enumerate([high, high, low]):
                    depth_ref[pl.ds(copy * depth + row * SIZE, SIZE), at] = value
            for more, panel in enumerate(later):
                value = carry_ref[pl.ds((count + more) * SIZE, SIZE), at] if carried else jnp.zeros((SIZE, wide), F32)
                refs[2 * count + 2][pl.ds(more * SIZE, SIZE), at] = less(value, panel, 1.0)

    left = left_depth(jnp.concatenate([ref[0] for ref in blocks], axis=1))
    for quarter in range(4):
        at = pl.ds(quarter * wide, wide)
        out_ref[:, at] = slab_ref[:, at] - dot(left, depth_ref[:, at])


def update(place, after, panels, left_over, sides, factors, slab, state, grams, carry):
    rows, columns = slab.shape
    steps = 4 if len(panels) > 1 else 2
    deep = rows // steps
    first, count = panels[0], len(panels)
    size = factors.shape[-1]
    groups = sorted({piece[1] for panel in panels for piece in pieces_of(panel)})
    strip = pl.BlockSpec((deep, columns), lambda j: (j, 0))
    specs, blocks = [], []
    for panel in panels:
        for side in range(2):
            specs.append(pl.BlockSpec((1, deep, LANES), lambda j, panel=panel: (panel, j, 0)))
            blocks.append(sides[side])
    factor = pl.BlockSpec((count, size, size), lambda j: (first // count, 0, 0), pipeline_mode=pl.Buffered(1))
    grams = grams if left_over or count > 1 else []
    carries = [] if carry is None else [carry]
    constant = [x for group in groups for x in state[group]] + list(grams) + carries
    outs, out_specs = [shape(rows, columns)], [strip]
    if left_over:
        outs.append(shape(left_over * size, columns))
        out_specs.append(pl.BlockSpec(outs[1].shape, lambda j: (0, 0)))
    made = pl.pallas_call(
        functools.partial(update_kernel, panels, len(grams), len(carries), left_over, len(after), groups),
        grid=(steps,),
        in_specs=[SMEM] + [ANY] * len(after) + [factor] + [whole(x) for x in constant] + specs + [strip],
        out_specs=out_specs,
        scratch_shapes=[pltpu.VMEM((3 * count * size, columns), jnp.bfloat16), pltpu.VMEM((count * size, columns), F32)],
        out_shape=outs,
        compiler_params=params(),
        cost_estimate=COST,
        name="update_panels" + "".join(map(str, panels)),
    )(place, *after, factors, *constant, *blocks, slab)
    return made[0], made[1] if left_over else None


def order_of(kind, bits):
    first, second = (0, 1) if kind == 0 else (1, 0)
    order = [first, 2, second] + list(range(3, bits)) if bits > 2 else [first, second]
    return order[:bits]


def swap(value, step):
    rows, cores = lax.axis_size("row"), lax.axis_size("col")
    bits = rows.bit_length() - 1
    pairs = [
        (row * cores + core, (row ^ (1 << order_of(core % 2, bits)[step])) * cores + core)
        for row in range(rows)
        for core in range(cores)
    ]
    return lax.ppermute(value, ("row", "col"), pairs)


def shift(value, step):
    count = lax.axis_size("col")
    return lax.ppermute(value, "col", [((target + step) % count, target) for target in range(count)])


def body(eigvecs, reflectors, factors):
    panels, _, width = reflectors.shape
    size = factors.shape[-1]
    others = size // width
    bits = lax.axis_size("row").bit_length() - 1
    slots = min(lax.axis_size("row"), eigvecs.shape[1] // LANES)
    cuts = slots.bit_length() - 1
    me, core = lax.axis_index("row"), lax.axis_index("col")
    own = [
        sum(((me >> bit) & 1) << (cuts - 1 - at) for at, bit in enumerate(order_of(kind, bits)[:cuts])) for kind in range(2)
    ]
    place = jnp.stack([jnp.where(core % 2 == 0, own[0], own[1])]).astype(jnp.int32)

    parts = [reflectors] + [shift(reflectors, step) for step in range(1, others)]
    join = lambda some: some[0] if len(some) == 1 else jnp.concatenate(some, axis=2)
    sides = [join(parts[: others // 2]), join(parts[others // 2 :])]
    factor_rows = jnp.concatenate([factors] + [shift(factors, step) for step in range(1, others)], axis=1)
    factors = lax.dynamic_slice_in_dim(jnp.concatenate([factor_rows, factor_rows], axis=2), core * width, size, axis=2)

    after = [jnp.zeros(TOKEN.shape, F32)]
    state, grams, slab, carry = {}, [], eigvecs, None

    def kernel(function, name, ins, outs):
        nonlocal after
        *made, token = small_call(function, name, after, place, ins, outs)
        after = [token]
        return made

    for event in schedule(bits + cuts - 1):
        if event[0] == "p":
            call = CALLS[int(event[1:])]
            after = after + ([factors] if event == "p1" else [])
            made, token = project(place, after, sides, call, eigvecs, grams if call == (GRAM_GROUP,) else [], slots)
            after = [token]
            for group, (keep, send) in zip(call, made):
                state[group] = [keep, swap(send, 0)]
        elif event == "g":
            rows, token = gram(place, after, reflectors, sides, slots)
            grams, after = [rows], [token]
        elif event[0] == "k":
            step, group = map(int, event[1:].split("."))
            held = state[group]
            wide, tall, _ = held[0].shape
            if step < cuts:
                keep, send = kernel(halve_kernel, f"halve{step}_{group}", held, [shape(wide // 2, tall, LANES)] * 2)
                state[group] = [keep, swap(send, step)]
            elif step <= bits:
                (total,) = kernel(add_kernel, f"sum{step}_{group}", held, [shape(*held[0].shape)])
                state[group] = [total, swap(total, step if step < bits else cuts - 1)]
            else:
                (block,) = kernel(join_kernel, f"join{step}_{group}", held, [shape(2 * wide, tall, LANES)])
                state[group] = [block, swap(block, cuts - 1 - (step - bits))]
        elif event[0] == "f":
            after = after + [state[int(event[2:])][1]]
        elif event == "x":
            wide = panels * (panels - 1) // 2 * size
            (rows,) = kernel(gram_rows_kernel, "gram_own", state[GRAM_GROUP], [shape(width, wide)])
            grams = [rows] + [shift(rows, step) for step in range(1, others)]
        else:
            some = UPDATES[int(event[1:])]
            slab, carry = update(
                place, after, some, panels - 1 - some[-1], sides, factors, slab, state, grams, carry
            )
            after = [slab]
    return slab


def solution(mesh):
    in_specs = (P("row", "col"), P(None, "row", "col"), P(None, "col", None))
    out_specs = P("row", "col")
    return jax.shard_map(body, mesh=mesh, in_specs=in_specs, out_specs=out_specs, check_vma=False)
```

```python
import functools

import jax
import jax.numpy as jnp
from jax import lax
from jax.experimental import pallas as pl
from jax.experimental.pallas import tpu as pltpu
from jax.sharding import PartitionSpec as P

LANES = 128
SIZE = 2 * LANES
VMEM_LIMIT = 40 * 1024 * 1024
FIRST_LIMIT = 58 * 1024 * 1024
PAIR_LIMIT = 48 * 1024 * 1024
F32 = jnp.float32

GROUPS = (
    ((0, 0, 0, 128), (1, 0, 0, 128)),
    ((0, 1, 0, 128), (1, 1, 0, 128)),
    ((2, 0, 0, 128), (2, 1, 0, 128)),
    ((3, 0, 0, 128), (3, 1, 0, 128)),
)
GRAM_GROUP = 1
CALLS = ((0,), (1,), (2,), (3,))
UPDATES = ((0, 1), (2,), (3,))
ORDER = (
    ["p0", "g", "p1", "k1.0", "p2", "k2.0", "p3", "k1.1", "k3.0", "k1.2", "k2.1", "k1.3", "k4.0", "k3.1", "k2.2", "k5.0", "k3.2", "k4.1", "k6.0", "k2.3", "k5.1", "k4.2", "k3.3", "k6.1", "k5.2"]
    + ["k4.3", "k7.0", "k7.1", "k6.2", "k5.3", "f.0", "k6.3", "k7.2", "k7.3", "f.1", "x", "u0", "f.2", "u1", "f.3", "u2"]
)


def schedule(steps):
    if steps == 7:
        return ORDER
    groups = range(len(GROUPS))
    order = ["p0", "g"] + [f"p{call}" for call in range(1, len(CALLS))]
    order += [f"k{step}.{group}" for step in range(1, steps + 1) for group in groups]
    return order + ["x"] + [f"u{update}" for update in range(len(UPDATES))]


def rows_of(chunk):
    return sum(last - first for _, _, first, last in chunk)


def pieces_of(panel):
    found = []
    for group, chunk in enumerate(GROUPS):
        row = 0
        for some, side, first, last in chunk:
            if some == panel:
                found.append((side * LANES + first, group, row, last - first))
            row += last - first
    return sorted(found)


def halves(value):
    high = value.astype(jnp.bfloat16)
    low = (value - high.astype(F32)).astype(jnp.bfloat16)
    return high, low


def left_depth(value):
    high, low = halves(value)
    return jnp.concatenate([high, low, high], axis=1)


def right_depth(value):
    high, low = halves(value)
    return jnp.concatenate([high, high, low], axis=0)


def dot(left, right):
    return jnp.dot(left, right, preferred_element_type=F32)


def shape(*dims):
    return jax.ShapeDtypeStruct(dims, F32)


TOKEN = shape(8, LANES)
ANY = pl.BlockSpec(memory_space=pl.ANY)
SMEM = pl.BlockSpec(memory_space=pltpu.SMEM)

COST = pl.CostEstimate(flops=3*10**9, bytes_accessed=100, transcendentals=0)


def params(limit=VMEM_LIMIT):
    return pltpu.CompilerParams(vmem_limit_bytes=limit)


def whole(array):
    rank = len(array.shape)
    return pl.BlockSpec(array.shape, lambda *at: (0,) * rank, pipeline_mode=pl.Buffered(1))


def small_call(kernel, name, after, place, ins, outs):
    def run(place_ref, *refs):
        refs = refs[len(after) :]
        kernel(place_ref, refs[: len(ins)], refs[len(ins) : -1])
        refs[-1][...] = jnp.zeros(TOKEN.shape, F32)

    return pl.pallas_call(
        run,
        in_specs=[SMEM] + [ANY] * len(after) + [pl.BlockSpec(memory_space=pltpu.VMEM)] * len(ins),
        out_shape=list(outs) + [TOKEN],
        compiler_params=params(),
        cost_estimate=COST,
        name=name,
    )(place, *after, *ins)


def project_kernel(steps, call, blocks, skip, grams, place, *refs):
    block_refs, slab_ref, refs = refs[skip : skip + len(blocks)], refs[skip + len(blocks)], refs[skip + len(blocks) + 1 :]
    gram_refs, outs, token_out, total = refs[:grams], refs[grams:-2], refs[-2], refs[-1]
    step = pl.program_id(0)
    turned = {block: ref[0].T for block, ref in zip(blocks, block_refs)}
    left = left_depth(
        jnp.concatenate([turned[panel, side][first:last] for group in call for panel, side, first, last in GROUPS[group]])
    )
    wide = slab_ref.shape[1] // 4
    for quarter in range(4):
        at = pl.ds(quarter * wide, wide)
        made = dot(left, right_depth(slab_ref[:, at]))

        @pl.when(step == 0)
        def _():
            total[:, at] = made

        @pl.when(step > 0)
        def _():
            total[:, at] += made

    @pl.when(step == steps - 1)
    def _():
        token_out[...] = jnp.zeros(TOKEN.shape, F32)
        half = outs[0].shape[0]
        above = 0
        for at, group in enumerate(call):
            tall = rows_of(GROUPS[group])
            for slot in range(2 * half):
                out = outs[2 * at + slot // half]
                lanes = pl.ds(pl.multiple_of((place[0] ^ slot) * LANES, LANES), LANES)
                out[slot % half, :tall] = total[pl.ds(above, tall), lanes]
                if gram_refs:
                    out[slot % half, tall:] = gram_refs[0][slot]
            above += tall


def project(place, after, sides, call, slab, grams, slots):
    rows, columns = slab.shape
    steps = 2
    deep = rows // steps
    above = sum(rows_of(GROUPS[group]) for group in call)
    halves_of = []
    for group in call:
        tall = rows_of(GROUPS[group]) + sum(x.shape[1] for x in grams)
        halves_of += [shape(slots // 2, tall, LANES)] * 2
    blocks = sorted({(panel, side) for group in call for panel, side, _, _ in GROUPS[group]})
    specs = [pl.BlockSpec((1, deep, LANES), lambda j, panel=panel: (panel, j, 0)) for panel, _ in blocks]
    strip = pl.BlockSpec((deep, columns), lambda j: (j, 0))
    out = pl.pallas_call(
        functools.partial(project_kernel, steps, call, blocks, len(after), len(grams)),
        grid=(steps,),
        in_specs=[SMEM] + [ANY] * len(after) + specs + [strip] + [whole(x) for x in grams],
        out_specs=[pl.BlockSpec(x.shape, lambda j: (0, 0, 0)) for x in halves_of]
        + [pl.BlockSpec(TOKEN.shape, lambda j: (0, 0))],
        scratch_shapes=[pltpu.VMEM((above, columns), F32)],
        out_shape=halves_of + [TOKEN],
        compiler_params=params(FIRST_LIMIT if call == CALLS[0] else VMEM_LIMIT),
        cost_estimate=COST,
        name="project_" + "".join(map(str, call)),
    )(place, *after, *[sides[side] for _, side in blocks], slab, *grams)
    return [(out[2 * at], out[2 * at + 1]) for at in range(len(call))], out[-1]


def gram_kernel(place, *refs):
    own_ref, side0_ref, side1_ref, out, token_out, rows_ref = refs[-6:]
    panels, _, width = own_ref.shape
    for other in range(panels - 1):
        left = jnp.concatenate([own_ref[panel].T for panel in range(other + 1, panels)])
        right = jnp.concatenate([side0_ref[other], side1_ref[other]], axis=1)
        made = dot(left_depth(left), right_depth(right))
        for row, panel in enumerate(range(other + 1, panels)):
            at = (panel * (panel - 1) // 2 + other) * SIZE
            rows_ref[:, pl.ds(at, SIZE)] = made[row * width : (row + 1) * width]
    slots = out.shape[0]
    tall = width // slots
    for slot in range(slots):
        rows = pl.ds(pl.multiple_of((place[0] ^ slot) * tall, tall), tall)
        for block in range(rows_ref.shape[1] // LANES):
            out[slot, pl.ds(block * tall, tall)] = rows_ref[rows, pl.ds(block * LANES, LANES)]
    token_out[...] = jnp.zeros(TOKEN.shape, F32)


def gram(place, after, reflectors, sides, slots):
    panels, _, width = reflectors.shape
    wide = panels * (panels - 1) // 2 * SIZE
    ins = [reflectors, *sides]
    return pl.pallas_call(
        gram_kernel,
        in_specs=[SMEM] + [ANY] * len(after) + [pl.BlockSpec(memory_space=pltpu.VMEM)] * 3,
        scratch_shapes=[pltpu.VMEM((width, wide), F32)],
        out_shape=[shape(slots, width // slots * (wide // LANES), LANES), TOKEN],
        compiler_params=params(),
        cost_estimate=COST,
        name="gram_rows",
    )(place, *after, *ins)


def gram_rows_kernel(place, ins, outs):
    (out,) = outs
    above = rows_of(GROUPS[GRAM_GROUP])
    half = ins[0].shape[0]
    tall = out.shape[0] // (2 * half)
    for slot in range(2 * half):
        rows = pl.ds(pl.multiple_of((place[0] ^ slot) * tall, tall), tall)
        for block in range(out.shape[1] // LANES):
            out[rows, pl.ds(block * LANES, LANES)] = ins[slot // half][slot % half, pl.ds(above + block * tall, tall)]


def halve_kernel(place, ins, outs):
    keep, got = ins
    half = outs[0].shape[0]
    outs[0][...] = keep[:half] + got[:half]
    outs[1][...] = keep[half:] + got[half:]


def add_kernel(place, ins, outs):
    outs[0][...] = ins[0][...] + ins[1][...]


def join_kernel(place, ins, outs):
    half = ins[0].shape[0]
    outs[0][:half] = ins[0][...]
    outs[0][half:] = ins[1][...]


def update_kernel(panels, parts, carried, left_over, skip, groups, place, *refs):
    count = len(panels)
    factor_ref, refs = refs[skip], refs[skip + 1 :]
    summed = {group: refs[2 * at : 2 * at + 2] for at, group in enumerate(groups)}
    refs = refs[2 * len(groups) :]
    gram_refs, refs = refs[:parts], refs[parts:]
    carry_ref, refs = (refs[0], refs[1:]) if carried else (None, refs)
    blocks, slab_ref, out_ref = refs[: 2 * count], refs[2 * count], refs[2 * count + 1]
    depth_ref, proj_ref = refs[-2:]
    depth = count * SIZE
    columns = slab_ref.shape[1]
    wide = columns // 4

    def gram_block(panel, other):
        at = pl.ds((panel * (panel - 1) // 2 + other) * SIZE, SIZE)
        width = gram_refs[0].shape[0]
        rows = [ref[:, at] for ref in gram_refs]
        return jnp.concatenate([pltpu.roll(part, step * width, 1) if step else part for step, part in enumerate(rows)])

    @pl.when(pl.program_id(0) == 0)
    def _():
        for row, panel in enumerate(panels):
            for at, group, first, tall in pieces_of(panel):
                half = summed[group][0].shape[0]
                for slot in range(2 * half):
                    lanes = pl.ds(pl.multiple_of((place[0] ^ slot) * LANES, LANES), LANES)
                    proj_ref[pl.ds(row * SIZE + at, tall), lanes] = summed[group][slot // half][
                        slot % half, pl.ds(first, tall)
                    ]
        factor = [left_depth(factor_ref[row]) for row in range(count)]
        later = [panels[-1] + 1 + more for more in range(left_over)]
        grams = {
            (panel, row): left_depth(gram_block(panel, panels[row]))
            for panel in list(panels) + later
            for row in range(count)
            if panels[row] < panel
        }
        for quarter in range(4):
            at = pl.ds(quarter * wide, wide)
            past = []

            def less(value, panel, sign):
                for row, weights in enumerate(past):
                    value = value + sign * dot(grams[panel, row], weights)
                return value

            for row in range(count):
                proj = proj_ref[pl.ds(row * SIZE, SIZE), at]
                if carried:
                    proj = proj - carry_ref[pl.ds(row * SIZE, SIZE), at]
                proj = less(proj, panels[row], -1.0)
                high, low = halves(dot(factor[row], right_depth(proj)))
                past.append(jnp.concatenate([high, high, low]))
                for copy, value in enumerate([high, high, low]):
                    depth_ref[pl.ds(copy * depth + row * SIZE, SIZE), at] = value
            for more, panel in enumerate(later):
                value = carry_ref[pl.ds((count + more) * SIZE, SIZE), at] if carried else jnp.zeros((SIZE, wide), F32)
                refs[2 * count + 2][pl.ds(more * SIZE, SIZE), at] = less(value, panel, 1.0)

    left = left_depth(jnp.concatenate([ref[0] for ref in blocks], axis=1))
    for quarter in range(4):
        at = pl.ds(quarter * wide, wide)
        out_ref[:, at] = slab_ref[:, at] - dot(left, depth_ref[:, at])


def update(place, after, panels, left_over, sides, factors, slab, state, grams, carry):
    rows, columns = slab.shape
    steps = 2
    deep = rows // steps
    first, count = panels[0], len(panels)
    size = factors.shape[-1]
    groups = sorted({piece[1] for panel in panels for piece in pieces_of(panel)})
    strip = pl.BlockSpec((deep, columns), lambda j: (j, 0))
    specs, blocks = [], []
    for panel in panels:
        for side in range(2):
            specs.append(pl.BlockSpec((1, deep, LANES), lambda j, panel=panel: (panel, j, 0)))
            blocks.append(sides[side])
    factor = pl.BlockSpec((count, size, size), lambda j: (first // count, 0, 0), pipeline_mode=pl.Buffered(1))
    grams = grams if left_over or count > 1 else []
    carries = [] if carry is None else [carry]
    constant = [x for group in groups for x in state[group]] + list(grams) + carries
    outs, out_specs = [shape(rows, columns)], [strip]
    if left_over:
        outs.append(shape(left_over * size, columns))
        out_specs.append(pl.BlockSpec(outs[1].shape, lambda j: (0, 0)))
    made = pl.pallas_call(
        functools.partial(update_kernel, panels, len(grams), len(carries), left_over, len(after), groups),
        grid=(steps,),
        in_specs=[SMEM] + [ANY] * len(after) + [factor] + [whole(x) for x in constant] + specs + [strip],
        out_specs=out_specs,
        scratch_shapes=[pltpu.VMEM((3 * count * size, columns), jnp.bfloat16), pltpu.VMEM((count * size, columns), F32)],
        out_shape=outs,
        compiler_params=params(PAIR_LIMIT if count > 1 else VMEM_LIMIT),
        cost_estimate=COST,
        name="update_panels" + "".join(map(str, panels)),
    )(place, *after, factors, *constant, *blocks, slab)
    return made[0], made[1] if left_over else None


def order_of(kind, bits):
    first, second = (0, 1) if kind == 0 else (1, 0)
    order = [first, 2, second] + list(range(3, bits)) if bits > 2 else [first, second]
    return order[:bits]


def swap(value, step):
    rows, cores = lax.axis_size("row"), lax.axis_size("col")
    bits = rows.bit_length() - 1
    pairs = [
        (row * cores + core, (row ^ (1 << order_of(core % 2, bits)[step])) * cores + core)
        for row in range(rows)
        for core in range(cores)
    ]
    return lax.ppermute(value, ("row", "col"), pairs)


def shift(value, step):
    count = lax.axis_size("col")
    return lax.ppermute(value, "col", [((target + step) % count, target) for target in range(count)])


def body(eigvecs, reflectors, factors):
    panels, _, width = reflectors.shape
    size = factors.shape[-1]
    others = size // width
    bits = lax.axis_size("row").bit_length() - 1
    slots = min(lax.axis_size("row"), eigvecs.shape[1] // LANES)
    cuts = slots.bit_length() - 1
    me, core = lax.axis_index("row"), lax.axis_index("col")
    own = [
        sum(((me >> bit) & 1) << (cuts - 1 - at) for at, bit in enumerate(order_of(kind, bits)[:cuts])) for kind in range(2)
    ]
    place = jnp.stack([jnp.where(core % 2 == 0, own[0], own[1])]).astype(jnp.int32)

    parts = [reflectors] + [shift(reflectors, step) for step in range(1, others)]
    join = lambda some: some[0] if len(some) == 1 else jnp.concatenate(some, axis=2)
    sides = [join(parts[: others // 2]), join(parts[others // 2 :])]
    factor_rows = jnp.concatenate([factors] + [shift(factors, step) for step in range(1, others)], axis=1)
    factors = lax.dynamic_slice_in_dim(jnp.concatenate([factor_rows, factor_rows], axis=2), core * width, size, axis=2)

    after = [jnp.zeros(TOKEN.shape, F32)]
    state, grams, slab, carry = {}, [], eigvecs, None

    def kernel(function, name, ins, outs):
        nonlocal after
        *made, token = small_call(function, name, after, place, ins, outs)
        after = [token]
        return made

    for event in schedule(bits + cuts - 1):
        if event[0] == "p":
            call = CALLS[int(event[1:])]
            after = after + ([factors] if event == "p1" else [])
            made, token = project(place, after, sides, call, eigvecs, grams if call == (GRAM_GROUP,) else [], slots)
            after = [token]
            for group, (keep, send) in zip(call, made):
                state[group] = [keep, swap(send, 0)]
        elif event == "g":
            rows, token = gram(place, after, reflectors, sides, slots)
            grams, after = [rows], [token]
        elif event[0] == "k":
            step, group = map(int, event[1:].split("."))
            held = state[group]
            wide, tall, _ = held[0].shape
            if step < cuts:
                keep, send = kernel(halve_kernel, f"halve{step}_{group}", held, [shape(wide // 2, tall, LANES)] * 2)
                state[group] = [keep, swap(send, step)]
            elif step <= bits:
                (total,) = kernel(add_kernel, f"sum{step}_{group}", held, [shape(*held[0].shape)])
                state[group] = [total, swap(total, step if step < bits else cuts - 1)]
            else:
                (block,) = kernel(join_kernel, f"join{step}_{group}", held, [shape(2 * wide, tall, LANES)])
                state[group] = [block, swap(block, cuts - 1 - (step - bits))]
        elif event[0] == "f":
            after = after + [state[int(event[2:])][1]]
        elif event == "x":
            wide = panels * (panels - 1) // 2 * size
            (rows,) = kernel(gram_rows_kernel, "gram_own", state[GRAM_GROUP], [shape(width, wide)])
            grams = [rows] + [shift(rows, step) for step in range(1, others)]
        else:
            some = UPDATES[int(event[1:])]
            slab, carry = update(
                place, after, some, panels - 1 - some[-1], sides, factors, slab, state, grams, carry
            )
            after = [slab]
    return slab


def solution(mesh):
    in_specs = (P("row", "col"), P(None, "row", "col"), P(None, "col", None))
    out_specs = P("row", "col")
    return jax.shard_map(body, mesh=mesh, in_specs=in_specs, out_specs=out_specs, check_vma=False)
```

```python
import functools

import jax
import jax.numpy as jnp
from jax import lax
from jax.experimental import pallas as pl
from jax.experimental.pallas import tpu as pltpu
from jax.sharding import PartitionSpec as P

LANES = 128
SIZE = 2 * LANES
VMEM_LIMIT = 40 * 1024 * 1024
FIRST_LIMIT = 58 * 1024 * 1024
F32 = jnp.float32

GROUPS = (
    ((0, 0, 0, 128), (1, 0, 0, 128)),
    ((0, 1, 0, 128), (1, 1, 0, 128)),
    ((2, 0, 0, 128), (2, 1, 0, 128)),
    ((3, 0, 0, 128), (3, 1, 0, 128)),
)
GRAM_GROUP = 1
CALLS = ((0,), (1,), (2,), (3,))
UPDATES = ((0, 1), (2,), (3,))
ORDER = (
    ["p0", "g", "p1", "k1.0", "p2", "k2.0", "p3", "k1.1", "k3.0", "k1.2", "k2.1", "k1.3", "k4.0", "k3.1", "k2.2", "k5.0", "k3.2", "k4.1", "k6.0", "k2.3", "k5.1", "k4.2", "k3.3", "k6.1", "k5.2"]
    + ["k4.3", "k7.0", "k7.1", "k6.2", "k5.3", "f.0", "k6.3", "k7.2", "k7.3", "f.1", "x", "u0", "f.2", "u1", "f.3", "u2"]
)


def schedule(steps):
    if steps == 7:
        return ORDER
    groups = range(len(GROUPS))
    order = ["p0", "g"] + [f"p{call}" for call in range(1, len(CALLS))]
    order += [f"k{step}.{group}" for step in range(1, steps + 1) for group in groups]
    return order + ["x"] + [f"u{update}" for update in range(len(UPDATES))]


def rows_of(chunk):
    return sum(last - first for _, _, first, last in chunk)


def pieces_of(panel):
    found = []
    for group, chunk in enumerate(GROUPS):
        row = 0
        for some, side, first, last in chunk:
            if some == panel:
                found.append((side * LANES + first, group, row, last - first))
            row += last - first
    return sorted(found)


def halves(value):
    high = value.astype(jnp.bfloat16)
    low = (value - high.astype(F32)).astype(jnp.bfloat16)
    return high, low


def left_depth(value):
    high, low = halves(value)
    return jnp.concatenate([high, low, high], axis=1)


def right_depth(value):
    high, low = halves(value)
    return jnp.concatenate([high, high, low], axis=0)


def dot(left, right):
    return jnp.dot(left, right, preferred_element_type=F32)


def shape(*dims):
    return jax.ShapeDtypeStruct(dims, F32)


TOKEN = shape(8, LANES)
ANY = pl.BlockSpec(memory_space=pl.ANY)
SMEM = pl.BlockSpec(memory_space=pltpu.SMEM)

COST = pl.CostEstimate(flops=3*10**9, bytes_accessed=100, transcendentals=0)


def params(limit=VMEM_LIMIT):
    return pltpu.CompilerParams(vmem_limit_bytes=limit)


def whole(array):
    rank = len(array.shape)
    return pl.BlockSpec(array.shape, lambda *at: (0,) * rank, pipeline_mode=pl.Buffered(1))


def small_call(kernel, name, after, place, ins, outs):
    def run(place_ref, *refs):
        refs = refs[len(after) :]
        kernel(place_ref, refs[: len(ins)], refs[len(ins) : -1])
        refs[-1][...] = jnp.zeros(TOKEN.shape, F32)

    return pl.pallas_call(
        run,
        in_specs=[SMEM] + [ANY] * len(after) + [pl.BlockSpec(memory_space=pltpu.VMEM)] * len(ins),
        out_shape=list(outs) + [TOKEN],
        compiler_params=params(),
        cost_estimate=COST,
        name=name,
    )(place, *after, *ins)


def project_kernel(steps, call, blocks, skip, grams, place, *refs):
    block_refs, slab_ref, refs = refs[skip : skip + len(blocks)], refs[skip + len(blocks)], refs[skip + len(blocks) + 1 :]
    gram_refs, outs, token_out, total = refs[:grams], refs[grams:-2], refs[-2], refs[-1]
    step = pl.program_id(0)
    turned = {block: ref[0].T for block, ref in zip(blocks, block_refs)}
    left = left_depth(
        jnp.concatenate([turned[panel, side][first:last] for group in call for panel, side, first, last in GROUPS[group]])
    )
    wide = slab_ref.shape[1] // 4
    for quarter in range(4):
        at = pl.ds(quarter * wide, wide)
        made = dot(left, right_depth(slab_ref[:, at]))

        @pl.when(step == 0)
        def _():
            total[:, at] = made

        @pl.when(step > 0)
        def _():
            total[:, at] += made

    @pl.when(step == steps - 1)
    def _():
        token_out[...] = jnp.zeros(TOKEN.shape, F32)
        half = outs[0].shape[0]
        above = 0
        for at, group in enumerate(call):
            tall = rows_of(GROUPS[group])
            for slot in range(2 * half):
                out = outs[2 * at + slot // half]
                lanes = pl.ds(pl.multiple_of((place[0] ^ slot) * LANES, LANES), LANES)
                out[slot % half, :tall] = total[pl.ds(above, tall), lanes]
                if gram_refs:
                    out[slot % half, tall:] = gram_refs[0][slot]
            above += tall


def project(place, after, sides, call, slab, grams, slots):
    rows, columns = slab.shape
    steps = 4 if call == CALLS[0] else 2
    deep = rows // steps
    above = sum(rows_of(GROUPS[group]) for group in call)
    halves_of = []
    for group in call:
        tall = rows_of(GROUPS[group]) + sum(x.shape[1] for x in grams)
        halves_of += [shape(slots // 2, tall, LANES)] * 2
    blocks = sorted({(panel, side) for group in call for panel, side, _, _ in GROUPS[group]})
    specs = [pl.BlockSpec((1, deep, LANES), lambda j, panel=panel: (panel, j, 0)) for panel, _ in blocks]
    strip = pl.BlockSpec((deep, columns), lambda j: (j, 0))
    out = pl.pallas_call(
        functools.partial(project_kernel, steps, call, blocks, len(after), len(grams)),
        grid=(steps,),
        in_specs=[SMEM] + [ANY] * len(after) + specs + [strip] + [whole(x) for x in grams],
        out_specs=[pl.BlockSpec(x.shape, lambda j: (0, 0, 0)) for x in halves_of]
        + [pl.BlockSpec(TOKEN.shape, lambda j: (0, 0))],
        scratch_shapes=[pltpu.VMEM((above, columns), F32)],
        out_shape=halves_of + [TOKEN],
        compiler_params=params(FIRST_LIMIT if call == CALLS[0] else VMEM_LIMIT),
        cost_estimate=COST,
        name="project_" + "".join(map(str, call)),
    )(place, *after, *[sides[side] for _, side in blocks], slab, *grams)
    return [(out[2 * at], out[2 * at + 1]) for at in range(len(call))], out[-1]


def gram_kernel(place, *refs):
    own_ref, side0_ref, side1_ref, out, token_out, rows_ref = refs[-6:]
    panels, _, width = own_ref.shape
    for other in range(panels - 1):
        left = jnp.concatenate([own_ref[panel].T for panel in range(other + 1, panels)])
        right = jnp.concatenate([side0_ref[other], side1_ref[other]], axis=1)
        made = dot(left_depth(left), right_depth(right))
        for row, panel in enumerate(range(other + 1, panels)):
            at = (panel * (panel - 1) // 2 + other) * SIZE
            rows_ref[:, pl.ds(at, SIZE)] = made[row * width : (row + 1) * width]
    slots = out.shape[0]
    tall = width // slots
    for slot in range(slots):
        rows = pl.ds(pl.multiple_of((place[0] ^ slot) * tall, tall), tall)
        for block in range(rows_ref.shape[1] // LANES):
            out[slot, pl.ds(block * tall, tall)] = rows_ref[rows, pl.ds(block * LANES, LANES)]
    token_out[...] = jnp.zeros(TOKEN.shape, F32)


def gram(place, after, reflectors, sides, slots):
    panels, _, width = reflectors.shape
    wide = panels * (panels - 1) // 2 * SIZE
    ins = [reflectors, *sides]
    return pl.pallas_call(
        gram_kernel,
        in_specs=[SMEM] + [ANY] * len(after) + [pl.BlockSpec(memory_space=pltpu.VMEM)] * 3,
        scratch_shapes=[pltpu.VMEM((width, wide), F32)],
        out_shape=[shape(slots, width // slots * (wide // LANES), LANES), TOKEN],
        compiler_params=params(),
        cost_estimate=COST,
        name="gram_rows",
    )(place, *after, *ins)


def gram_rows_kernel(place, ins, outs):
    (out,) = outs
    above = rows_of(GROUPS[GRAM_GROUP])
    half = ins[0].shape[0]
    tall = out.shape[0] // (2 * half)
    for slot in range(2 * half):
        rows = pl.ds(pl.multiple_of((place[0] ^ slot) * tall, tall), tall)
        for block in range(out.shape[1] // LANES):
            out[rows, pl.ds(block * LANES, LANES)] = ins[slot // half][slot % half, pl.ds(above + block * tall, tall)]


def halve_kernel(place, ins, outs):
    keep, got = ins
    half = outs[0].shape[0]
    outs[0][...] = keep[:half] + got[:half]
    outs[1][...] = keep[half:] + got[half:]


def add_kernel(place, ins, outs):
    outs[0][...] = ins[0][...] + ins[1][...]


def join_kernel(place, ins, outs):
    half = ins[0].shape[0]
    outs[0][:half] = ins[0][...]
    outs[0][half:] = ins[1][...]


def update_kernel(panels, parts, carried, left_over, skip, groups, place, *refs):
    count = len(panels)
    factor_ref, refs = refs[skip], refs[skip + 1 :]
    summed = {group: refs[2 * at : 2 * at + 2] for at, group in enumerate(groups)}
    refs = refs[2 * len(groups) :]
    gram_refs, refs = refs[:parts], refs[parts:]
    carry_ref, refs = (refs[0], refs[1:]) if carried else (None, refs)
    blocks, slab_ref, out_ref = refs[: 2 * count], refs[2 * count], refs[2 * count + 1]
    depth_ref, proj_ref = refs[-2:]
    depth = count * SIZE
    columns = slab_ref.shape[1]
    wide = columns // 4

    def gram_block(panel, other):
        at = pl.ds((panel * (panel - 1) // 2 + other) * SIZE, SIZE)
        width = gram_refs[0].shape[0]
        rows = [ref[:, at] for ref in gram_refs]
        return jnp.concatenate([pltpu.roll(part, step * width, 1) if step else part for step, part in enumerate(rows)])

    @pl.when(pl.program_id(0) == 0)
    def _():
        for row, panel in enumerate(panels):
            for at, group, first, tall in pieces_of(panel):
                half = summed[group][0].shape[0]
                for slot in range(2 * half):
                    lanes = pl.ds(pl.multiple_of((place[0] ^ slot) * LANES, LANES), LANES)
                    proj_ref[pl.ds(row * SIZE + at, tall), lanes] = summed[group][slot // half][
                        slot % half, pl.ds(first, tall)
                    ]
        factor = [left_depth(factor_ref[row]) for row in range(count)]
        later = [panels[-1] + 1 + more for more in range(left_over)]
        grams = {
            (panel, row): left_depth(gram_block(panel, panels[row]))
            for panel in list(panels) + later
            for row in range(count)
            if panels[row] < panel
        }
        for quarter in range(4):
            at = pl.ds(quarter * wide, wide)
            past = []

            def less(value, panel, sign):
                for row, weights in enumerate(past):
                    value = value + sign * dot(grams[panel, row], weights)
                return value

            for row in range(count):
                proj = proj_ref[pl.ds(row * SIZE, SIZE), at]
                if carried:
                    proj = proj - carry_ref[pl.ds(row * SIZE, SIZE), at]
                proj = less(proj, panels[row], -1.0)
                high, low = halves(dot(factor[row], right_depth(proj)))
                past.append(jnp.concatenate([high, high, low]))
                for copy, value in enumerate([high, high, low]):
                    depth_ref[pl.ds(copy * depth + row * SIZE, SIZE), at] = value
            for more, panel in enumerate(later):
                value = carry_ref[pl.ds((count + more) * SIZE, SIZE), at] if carried else jnp.zeros((SIZE, wide), F32)
                refs[2 * count + 2][pl.ds(more * SIZE, SIZE), at] = less(value, panel, 1.0)

    left = left_depth(jnp.concatenate([ref[0] for ref in blocks], axis=1))
    for quarter in range(4):
        at = pl.ds(quarter * wide, wide)
        out_ref[:, at] = slab_ref[:, at] - dot(left, depth_ref[:, at])


def update(place, after, panels, left_over, sides, factors, slab, state, grams, carry):
    rows, columns = slab.shape
    steps = 4 if len(panels) > 1 else 2
    deep = rows // steps
    first, count = panels[0], len(panels)
    size = factors.shape[-1]
    groups = sorted({piece[1] for panel in panels for piece in pieces_of(panel)})
    strip = pl.BlockSpec((deep, columns), lambda j: (j, 0))
    specs, blocks = [], []
    for panel in panels:
        for side in range(2):
            specs.append(pl.BlockSpec((1, deep, LANES), lambda j, panel=panel: (panel, j, 0)))
            blocks.append(sides[side])
    factor = pl.BlockSpec((count, size, size), lambda j: (first // count, 0, 0), pipeline_mode=pl.Buffered(1))
    grams = grams if left_over or count > 1 else []
    carries = [] if carry is None else [carry]
    constant = [x for group in groups for x in state[group]] + list(grams) + carries
    outs, out_specs = [shape(rows, columns)], [strip]
    if left_over:
        outs.append(shape(left_over * size, columns))
        out_specs.append(pl.BlockSpec(outs[1].shape, lambda j: (0, 0)))
    made = pl.pallas_call(
        functools.partial(update_kernel, panels, len(grams), len(carries), left_over, len(after), groups),
        grid=(steps,),
        in_specs=[SMEM] + [ANY] * len(after) + [factor] + [whole(x) for x in constant] + specs + [strip],
        out_specs=out_specs,
        scratch_shapes=[pltpu.VMEM((3 * count * size, columns), jnp.bfloat16), pltpu.VMEM((count * size, columns), F32)],
        out_shape=outs,
        compiler_params=params(),
        cost_estimate=COST,
        name="update_panels" + "".join(map(str, panels)),
    )(place, *after, factors, *constant, *blocks, slab)
    return made[0], made[1] if left_over else None


def order_of(kind, bits):
    first, second = (0, 1) if kind == 0 else (1, 0)
    order = [first, 2, second] + list(range(3, bits)) if bits > 2 else [first, second]
    return order[:bits]


def swap(value, step):
    rows, cores = lax.axis_size("row"), lax.axis_size("col")
    bits = rows.bit_length() - 1
    pairs = [
        (row * cores + core, (row ^ (1 << order_of(core % 2, bits)[step])) * cores + core)
        for row in range(rows)
        for core in range(cores)
    ]
    return lax.ppermute(value, ("row", "col"), pairs)


def shift(value, step):
    count = lax.axis_size("col")
    return lax.ppermute(value, "col", [((target + step) % count, target) for target in range(count)])


def body(eigvecs, reflectors, factors):
    panels, _, width = reflectors.shape
    size = factors.shape[-1]
    others = size // width
    bits = lax.axis_size("row").bit_length() - 1
    slots = min(lax.axis_size("row"), eigvecs.shape[1] // LANES)
    cuts = slots.bit_length() - 1
    me, core = lax.axis_index("row"), lax.axis_index("col")
    own = [
        sum(((me >> bit) & 1) << (cuts - 1 - at) for at, bit in enumerate(order_of(kind, bits)[:cuts])) for kind in range(2)
    ]
    place = jnp.stack([jnp.where(core % 2 == 0, own[0], own[1])]).astype(jnp.int32)

    parts = [reflectors] + [shift(reflectors, step) for step in range(1, others)]
    join = lambda some: some[0] if len(some) == 1 else jnp.concatenate(some, axis=2)
    sides = [join(parts[: others // 2]), join(parts[others // 2 :])]
    factor_rows = jnp.concatenate([factors] + [shift(factors, step) for step in range(1, others)], axis=1)
    factors = lax.dynamic_slice_in_dim(jnp.concatenate([factor_rows, factor_rows], axis=2), core * width, size, axis=2)

    after = [jnp.zeros(TOKEN.shape, F32)]
    state, grams, slab, carry = {}, [], eigvecs, None

    def kernel(function, name, ins, outs):
        nonlocal after
        *made, token = small_call(function, name, after, place, ins, outs)
        after = [token]
        return made

    for event in schedule(bits + cuts - 1):
        if event[0] == "p":
            call = CALLS[int(event[1:])]
            after = after + ([factors] if event == "p1" else [])
            made, token = project(place, after, sides, call, eigvecs, grams if call == (GRAM_GROUP,) else [], slots)
            after = [token]
            for group, (keep, send) in zip(call, made):
                state[group] = [keep, swap(send, 0)]
        elif event == "g":
            rows, token = gram(place, after, reflectors, sides, slots)
            grams, after = [rows], [token]
        elif event[0] == "k":
            step, group = map(int, event[1:].split("."))
            held = state[group]
            wide, tall, _ = held[0].shape
            if step < cuts:
                keep, send = kernel(halve_kernel, f"halve{step}_{group}", held, [shape(wide // 2, tall, LANES)] * 2)
                state[group] = [keep, swap(send, step)]
            elif step <= bits:
                (total,) = kernel(add_kernel, f"sum{step}_{group}", held, [shape(*held[0].shape)])
                state[group] = [total, swap(total, step if step < bits else cuts - 1)]
            else:
                (block,) = kernel(join_kernel, f"join{step}_{group}", held, [shape(2 * wide, tall, LANES)])
                state[group] = [block, swap(block, cuts - 1 - (step - bits))]
        elif event[0] == "f":
            after = after + [state[int(event[2:])][1]]
        elif event == "x":
            wide = panels * (panels - 1) // 2 * size
            (rows,) = kernel(gram_rows_kernel, "gram_own", state[GRAM_GROUP], [shape(width, wide)])
            grams = [rows] + [shift(rows, step) for step in range(1, others)]
        else:
            some = UPDATES[int(event[1:])]
            slab, carry = update(
                place, after, some, panels - 1 - some[-1], sides, factors, slab, state, grams, carry
            )
            after = [slab]
    return slab


def solution(mesh):
    in_specs = (P("row", "col"), P(None, "row", "col"), P(None, "col", None))
    out_specs = P("row", "col")
    return jax.shard_map(body, mesh=mesh, in_specs=in_specs, out_specs=out_specs, check_vma=False)
```
